512 devices in a mesh: state: 8 (over x, core), member: 64 (over z, y).
Axes of the slice: x: 4, y: 8, z: 8, core: 2. Of those that a mesh axis runs over, the one named last changes fastest.
Arguments:
- state: float32 [2048, 5120], P('member', 'state'), may hold values from -6 to 6
- obs_values: float32 [2, 384], replicated, may hold values from -8 to 8
- noise_var: float32 [2, 384], replicated, may hold values from 0.3 to 3
- obs_rows: int32 [2, 384], replicated, may hold values from 0 to 639
- owner: int32 [2, 3], replicated, may hold values from 0 to 7
Outputs:
- analysis: float32 [2048, 5120], P('member', 'state')
The draws below stay inside these ranges and needn't reach their ends.
All inputs are finite; a program needn't handle non-finite values.
Results may differ from the reference program's by a relative error of at most 0.0003.
Values sent between devices are 32-bit elements; how exact they have to be, the bound alone decides.
A program may use at most 64 MiB of HBM per device.

```python
import math
import jax
import jax.numpy as jnp
from jax import lax

ROWS_DEV = 640
MEMBERS = 2048
OBS = 384
TILE = 128
BLOCKS = 2
OBS_TILES = 3
NSTATE = 5120
N_STATE = 8


def with_ends(values, rng, smallest, top_value):
    longest = values.shape.index(max(values.shape))
    spots = []
    for shift in (0, 1):
        where = [jax.random.randint(jax.random.fold_in(rng, axis), (), 0, length) for axis, length in enumerate(values.shape)]
        where[longest] = (where[longest] + shift) % values.shape[longest]
        spots.append(tuple(where))
    return values.at[spots[0]].set(smallest).at[spots[1]].set(top_value)


def level_of(key, dims, split, least, high):
    def one(dim, parts):
        heights = jax.random.uniform(jax.random.fold_in(jax.random.fold_in(key, 6), dim), (parts,), jnp.float32, least / len(split), high / len(split))
        return jnp.repeat(jnp.exp(heights), dims[dim] // parts).reshape((-1,) + (1,) * (len(dims) - dim - 1))

    gain = one(*split[0])
    for cut in split[1:]:
        gain = gain * one(*cut)
    return gain


def bell_draw(key, dims, spread, limit, pieces=(), kind=jnp.bfloat16):
    result = jax.random.normal(key, dims, jnp.float32) * spread
    if len(pieces) > 0:
        result = level_of(key, dims, pieces, -0.22, 0.18) * result
    return jnp.clip(result, min=-limit, max=limit).astype(kind)


def setup_inputs(seed: int = 0) -> dict:
    splits = jax.random.split(jax.random.key(seed), 6)
    state = bell_draw(splits[0], (MEMBERS, NSTATE), 1.0, 6.0, ((0, 64), (1, 8)), jnp.float32)
    obs_values = bell_draw(splits[1], (BLOCKS, OBS), 1.5, 8.0, (), jnp.float32)
    noise_var = jnp.clip(jnp.exp(jax.random.uniform(splits[2], (BLOCKS, OBS), jnp.float32, math.log(0.3), math.log(3.0))), 0.3, 3.0)
    obs_rows = with_ends(jax.random.randint(splits[3], (BLOCKS, OBS), 0, ROWS_DEV), jax.random.fold_in(splits[3], 1), 0, ROWS_DEV - 1).astype(jnp.int32)
    owner = with_ends(jax.random.randint(splits[4], (BLOCKS, OBS_TILES), 0, N_STATE), jax.random.fold_in(splits[4], 1), 0, N_STATE - 1).astype(jnp.int32)
    return {"state": state, "obs_values": obs_values, "noise_var": noise_var, "obs_rows": obs_rows, "owner": owner}


def full_dot(left, right):
    return jnp.dot(left.astype(jnp.float32), right.astype(jnp.float32), precision=lax.Precision.HIGHEST, preferred_element_type=jnp.float32)

def solve_gram(factor, right):
    half = lax.linalg.triangular_solve(factor, right, left_side=True, lower=True)
    return lax.linalg.triangular_solve(factor, half, left_side=True, lower=True, transpose_a=True)

def analyse(current, observed, target, noise):
    count = current.shape[0]
    row_mean = jnp.sum(current, axis=0) / count
    obs_mean = jnp.sum(observed, axis=0) / count
    row_anom = current - row_mean[None, :]
    obs_anom = observed - obs_mean[None, :]
    cross = full_dot(obs_anom.T, row_anom) / (count - 1.0)
    innov_cov = full_dot(obs_anom.T, obs_anom) / (count - 1.0) + jnp.diag(noise)
    factor = jnp.linalg.cholesky(innov_cov)
    weights = solve_gram(factor, (target - obs_mean)[:, None])
    transformed = solve_gram(factor, obs_anom.T)
    shift = full_dot(weights.T, cross)
    return row_mean[None, :] + shift + row_anom - 0.5 * full_dot(transformed.T, cross)

def reference(state, obs_values, noise_var, obs_rows, owner):
    current = state
    for block in range(BLOCKS):
        owners_each = jnp.repeat(owner[block], TILE).astype(jnp.int32)
        picks = (owners_each * ROWS_DEV + obs_rows[block]).astype(jnp.int32)
        observed = jnp.take(current, picks, axis=1)
        current = analyse(current, observed, obs_values[block], noise_var[block])
    return current
```

```python
import functools

import jax
import jax.numpy as jnp
from jax import lax
from jax.experimental import pallas as pl
from jax.experimental.pallas import tpu as pltpu
from jax.sharding import PartitionSpec as P

MESH = pl.DeviceIdType.MESH
F32 = jnp.float32
HIGHEST = lax.Precision.HIGHEST
SIDE = 8
OBS = 384
ALL = 2 * OBS
ROWS = 640
MINE = 32
MEMBERS = 2048
BLOCKS = [(i, j) for i in range(6) for j in range(i + 1)]


def dot(a, b, over=(1, 0)):
    return lax.dot_general(
        a, b, (((over[0],), (over[1],)), ((), ())), precision=HIGHEST, preferred_element_type=F32
    )


def total(slots, own):
    out = own
    for k in range(1, SIDE):
        out = out + slots[k]
    return out


def gather_kernel(
    x_ref, l_ref, oa_ref, mean_ref, gram_ref, cross_ref,
    t_in, t_z, t_y, t_s, l_src, l_in, l_mine, l_all, anom,
    g_part, g_one, g_red, g_two, c_part, c_one, c_red, c_two, c_sum,
    t_send, t_recv, l_send, l_recv, g_send, g_recv, x_send, x_recv, c_send, c_recv,
):
    s = lax.axis_index("state")
    m = lax.axis_index("member")
    z, y = lax.div(m, SIDE), lax.rem(m, SIDE)
    xpos, core = lax.div(s, 2), lax.rem(s, 2)

    def hop(v, k):
        return lax.rem(v + k, SIDE)

    def peer(axis, k):
        if axis == "z":
            return (s, hop(z, k) * SIDE + y)
        if axis == "y":
            return (s, z * SIDE + hop(y, k))
        return (hop(s, k), m)

    barrier = pltpu.get_barrier_semaphore()
    for axis in ("z", "y", "s"):
        for k in range(1, SIDE):
            pl.semaphore_signal(barrier, inc=1, device_id=peer(axis, k), device_id_type=MESH)

    def copy(src, dst, send, recv, where):
        c = pltpu.make_async_remote_copy(
            src_ref=src, dst_ref=dst, send_sem=send, recv_sem=recv, device_id=where, device_id_type=MESH
        )
        c.start()
        return c

    def arrive(copies):
        for c in copies:
            c.wait_recv()

    started = []

    def fan(axis, src, dst, send, recv):
        out = [copy(src(k), dst(k), send.at[k], recv.at[k], peer(axis, k)) for k in range(1, SIDE)]
        started.extend(out)
        return out

    x = x_ref[...]
    lrows = l_ref[...]
    t_in[...] = jnp.zeros_like(t_in)
    sx = jnp.sum(x, axis=0, keepdims=True)
    sl = jnp.sum(lrows, axis=0, keepdims=True)
    for b in range(5):
        t_in[8 + b : 9 + b, :] = sx[:, 128 * b : 128 * b + 128]
    for b in range(6):
        t_in[b : b + 1, :] = sl[:, 128 * b : 128 * b + 128]
        l_src[4 * b : 4 * b + 4] = lrows[:, 128 * b : 128 * b + 128].reshape(4, 8, 128)
    pl.semaphore_wait(barrier, 3 * (SIDE - 1))

    tz = fan("z", lambda k: t_in, lambda k: t_z.at[k], t_send.at[0], t_recv.at[0])
    ls = fan("s", lambda k: l_src.at[pl.ds(3 * hop(s, k), 3)], lambda k: l_in.at[k], l_send.at[0], l_recv.at[0])
    arrive(ls)
    l_mine[...] = total(l_in, l_src[pl.ds(3 * s, 3)])
    l_all[pl.ds(3 * s, 3)] = l_mine[...]
    la = fan("s", lambda k: l_mine, lambda k: l_all.at[pl.ds(3 * s, 3)], l_send.at[1], l_recv.at[1])
    arrive(tz)
    t_y[0] = total(t_z, t_in[...])
    ty = fan("y", lambda k: t_y.at[0], lambda k: t_y.at[k], t_send.at[1], t_recv.at[1])
    arrive(ty)
    sums = total(t_y, t_y[0])
    t_s[0] = sums[0:8]
    ts = fan("s", lambda k: t_s.at[0], lambda k: t_s.at[k], t_send.at[2], t_recv.at[2])
    xmean = sums[8:16] / MEMBERS
    for b in range(5):
        anom[:, 128 * b : 128 * b + 128] = x[:, 128 * b : 128 * b + 128] - xmean[b : b + 1]
    arrive(la)
    arrive(ts)
    omean = total(t_s, t_s[0]) / MEMBERS
    mean_ref[...] = omean
    for b in range(6):
        oa_ref[:, 128 * b : 128 * b + 128] = l_all[4 * b : 4 * b + 4].reshape(MINE, 128) - omean[b : b + 1]

    for i in range(6):
        band = dot(oa_ref[:, 128 * i : 128 * i + 128], oa_ref[:, 0 : 128 * i + 128], (0, 0))
        for j in range(i + 1):
            at = 16 * BLOCKS.index((i, j))
            g_part[at : at + 16] = band[:, 128 * j : 128 * j + 128].reshape(16, 8, 128)
    g_part[336:384] = jnp.zeros((48, 8, 128), F32)

    gbase = s * 48
    order = (("z", z, "y", y), ("y", y, "z", z))
    g1 = []
    for h, (first, a, second, b) in enumerate(order):
        g1.append(
            fan(
                first,
                lambda k: g_part.at[pl.ds(gbase + 24 * h + 3 * hop(a, k), 3)],
                lambda k: g_one.at[h, k],
                g_send.at[h, 0],
                g_recv.at[h, 0],
            )
        )
    for i in range(6):
        band = dot(oa_ref[:, 128 * i : 128 * i + 128], anom[...], (0, 0))
        for j in range(5):
            at = 96 * j + 16 * i
            c_part[at : at + 16] = band[:, 128 * j : 128 * j + 128].reshape(16, 8, 128)
    c_part[480:512] = jnp.zeros((32, 8, 128), F32)

    g2 = []
    for h, (first, a, second, b) in enumerate(order):
        arrive(g1[h])
        g_two[h, 0] = total(g_one.at[h], g_part[pl.ds(gbase + 24 * h + 3 * a, 3)])
        g2.append(
            fan(second, lambda k: g_two.at[h, 0], lambda k: g_two.at[h, k], g_send.at[h, 1], g_recv.at[h, 1])
        )
    g3 = []
    for h, (first, a, second, b) in enumerate(order):
        arrive(g2[h])
        g_red[h] = total(g_two.at[h], g_two[h, 0])
        spot = pl.ds(gbase + 24 * h + 3 * a, 3)
        gram_ref[spot] = g_red[h]
        g3.append(
            fan(first, lambda k: g_red.at[h], lambda k: gram_ref.at[spot], g_send.at[h, 2], g_recv.at[h, 2])
        )
    arrive(g3[0])
    arrive(g3[1])
    mine = pl.ds(gbase, 48)
    gx = []
    for k in range(1, 4):
        where = (lax.rem(xpos + k, 4) * 2 + core, m)
        gx.append(copy(gram_ref.at[mine], gram_ref.at[mine], x_send.at[k], x_recv.at[k], where))
    started.extend(gx)
    gc = []
    for k in range(4):
        if k > 0:
            gx[k - 1].wait_recv()
        got = pl.ds((lax.rem(xpos + 4 - k, 4) * 2 + core) * 48, 48)
        gc.append(copy(gram_ref.at[got], gram_ref.at[got], x_send.at[4 + k], x_recv.at[4 + k], (s + 1 - 2 * core, m)))
    started.extend(gc)

    c1 = []
    for h, (first, a, second, b) in enumerate(order):
        c1.append(
            fan(
                first,
                lambda k: c_part.at[pl.ds(256 * h + 32 * hop(a, k), 32)],
                lambda k: c_one.at[h, k],
                c_send.at[h, 0],
                c_recv.at[h, 0],
            )
        )
    c2 = []
    for h, (first, a, second, b) in enumerate(order):
        arrive(c1[h])
        c_red[h] = total(c_one.at[h], c_part[pl.ds(256 * h + 32 * a, 32)])
        c2.append(
            fan(
                second,
                lambda k: c_red.at[h, pl.ds(4 * hop(b, k), 4)],
                lambda k: c_two.at[h, k],
                c_send.at[h, 1],
                c_recv.at[h, 1],
            )
        )
    c3 = []
    for h, (first, a, second, b) in enumerate(order):
        arrive(c2[h])
        c_two[h, 0] = total(c_two.at[h], c_red[h, pl.ds(4 * b, 4)])
        spot = pl.ds(4 * b, 4)
        c_sum[h, spot] = c_two[h, 0]
        c3.append(
            fan(second, lambda k: c_two.at[h, 0], lambda k: c_sum.at[h, spot], c_send.at[h, 2], c_recv.at[h, 2])
        )
    c4 = []
    for h, (first, a, second, b) in enumerate(order):
        arrive(c3[h])
        spot = pl.ds(256 * h + 32 * a, 32)
        cross_ref[spot] = c_sum[h]
        c4.append(
            fan(first, lambda k: c_sum.at[h], lambda k: cross_ref.at[spot], c_send.at[h, 3], c_recv.at[h, 3])
        )
    arrive(gc)
    arrive(c4[0])
    arrive(c4[1])
    for c in started:
        c.wait_send()


def gather_all(x, picked):
    dma = pltpu.SemaphoreType.DMA
    tiles = lambda *lead: pltpu.VMEM((*lead, 8, 128), F32)
    return pl.pallas_call(
        gather_kernel,
        out_shape=(
            jax.ShapeDtypeStruct((MINE, ALL), F32),
            jax.ShapeDtypeStruct((8, 128), F32),
            jax.ShapeDtypeStruct((384, 8, 128), F32),
            jax.ShapeDtypeStruct((512, 8, 128), F32),
        ),
        in_specs=[pl.BlockSpec(memory_space=pltpu.VMEM)] * 2,
        out_specs=[pl.BlockSpec(memory_space=pltpu.VMEM)] * 4,
        scratch_shapes=[
            pltpu.VMEM((16, 128), F32), pltpu.VMEM((SIDE, 16, 128), F32), pltpu.VMEM((SIDE, 16, 128), F32), tiles(SIDE),
            tiles(24), tiles(SIDE, 3), tiles(3), tiles(24), pltpu.VMEM((MINE, ROWS), F32),
            tiles(384), tiles(2, SIDE, 3), tiles(2, 3), tiles(2, SIDE, 3),
            tiles(512), tiles(2, SIDE, 32), tiles(2, 32), tiles(2, SIDE, 4), tiles(2, 32),
            dma((3, SIDE)), dma((3, SIDE)), dma((2, SIDE)), dma((2, SIDE)), dma((2, 3, SIDE)), dma((2, 3, SIDE)),
            dma((SIDE,)), dma((SIDE,)), dma((2, 4, SIDE)), dma((2, 4, SIDE)),
        ],
        compiler_params=pltpu.CompilerParams(
            collective_id=0, has_side_effects=True, vmem_limit_bytes=40 * 2**20
        ),
    )(x, picked)


def solve(factor, right):
    half = lax.linalg.triangular_solve(factor, right, left_side=True, lower=True)
    return lax.linalg.triangular_solve(factor, half, left_side=True, lower=True, transpose_a=True)


def shards(state, obs_values, noise_var, obs_rows, owner):
    s = lax.axis_index("state")
    held = jnp.repeat(owner.reshape(-1) == s, 128)
    picked = jnp.where(held[None, :], jnp.take(state, obs_rows.reshape(-1), axis=1), 0.0)
    oa, means, gram, cross = gather_all(state, picked)
    scale = 1.0 / (MEMBERS - 1.0)
    rows = []
    parts = gram[:336].reshape(21, 128, 128)
    for i in range(6):
        row = []
        for j in range(6):
            row.append(parts[BLOCKS.index((i, j))] if j <= i else parts[BLOCKS.index((j, i))].T)
        rows.append(jnp.concatenate(row, axis=1))
    gram = jnp.concatenate(rows, axis=0) * scale
    cross = cross[:480].reshape(5, ALL, 128).transpose(1, 0, 2).reshape(ALL, ROWS) * scale
    omean = means[:6].reshape(ALL)
    c12, c21 = gram[:OBS, OBS:], gram[OBS:, :OBS]
    gap = obs_values.reshape(-1) - omean
    f1 = jnp.linalg.cholesky(gram[:OBS, :OBS] + jnp.diag(noise_var[0]))
    u = solve(f1, c12)
    f = 0.75 * c21 + 0.25 * dot(u * noise_var[0][:, None], jnp.eye(OBS, dtype=F32), (0, 0))
    f2 = jnp.linalg.cholesky(gram[OBS:, OBS:] - dot(f, u) + jnp.diag(noise_var[1]))
    g1, g2 = gap[None, :OBS], gap[None, OBS:]
    o1, o2 = oa[:, :OBS], oa[:, OBS:]
    b1 = g1 - 0.5 * o1
    b2 = g2 - 0.5 * o2 - dot(g1 - 0.25 * o1, u)
    q2 = solve(f2, b2.T).T
    q1 = solve(f1, (b1 - dot(q2, f)).T).T
    return state + dot(q1, cross[:OBS]) + dot(q2, cross[OBS:])


def solution(mesh):
    placed = (P("member", "state"), P(), P(), P(), P())
    return jax.shard_map(
        shards, mesh=mesh, in_specs=placed, out_specs=P("member", "state"), check_vma=False
    )
```

```python
import functools

import jax
import jax.numpy as jnp
from jax import lax
from jax.experimental import pallas as pl
from jax.experimental.pallas import tpu as pltpu
from jax.sharding import PartitionSpec as P

MESH = pl.DeviceIdType.MESH
F32 = jnp.float32
HIGHEST = lax.Precision.HIGHEST
SIDE = 8
OBS = 384
ALL = 2 * OBS
ROWS = 640
MINE = 32
MEMBERS = 2048
BLOCKS = [(i, j) for i in range(6) for j in range(i + 1)]


def dot(a, b, over=(1, 0)):
    return lax.dot_general(
        a, b, (((over[0],), (over[1],)), ((), ())), precision=HIGHEST, preferred_element_type=F32
    )


def total(slots, own):
    out = own
    for k in range(1, SIDE):
        out = out + slots[k]
    return out


def eliminate(ref, at):
    spread = functools.partial(jnp.broadcast_to, shape=(8, 128))
    lane = lax.broadcasted_iota(jnp.int32, (8, 128), 1)
    sub = lax.broadcasted_iota(jnp.int32, (8, 128), 0)
    a = [ref[at + 8 * i : at + 8 * i + 8, at : at + 128] for i in range(16)]
    for p in range(16):
        rows = a[p]
        cols = [spread(rows[:, 8 * p + j : 8 * p + j + 1]) for j in range(8)]
        for k in range(8):
            col = cols[k]
            pivot = 1.0 / spread(col[k : k + 1])
            rows = jnp.where(lane == 8 * p + k, jnp.where(sub == k, 1.0, 0.0), rows)
            times = jnp.where(sub == k, 1.0 - pivot, col * pivot)
            for j in range(k + 1, 8):
                cols[j] = cols[j] - times * spread(cols[j][k : k + 1])
            rows = rows - times * spread(rows[k : k + 1])
        each = [spread(rows[j : j + 1]) for j in range(8)]
        inside = (lane >= 8 * p) & (lane < 8 * p + 8)
        for i in [(p + 1 + i) % 16 for i in range(15)]:
            old = a[i]
            t = [spread(old[:, 8 * p + j : 8 * p + j + 1]) * each[j] for j in range(8)]
            low, high = (t[0] + t[1]) + (t[2] + t[3]), (t[4] + t[5]) + (t[6] + t[7])
            a[i] = jnp.where(inside, 0.0, old) - (low + high)
        a[p] = rows
    for i in range(16):
        ref[at + 8 * i : at + 8 * i + 8, at : at + 128] = a[i]


def sweep(ref, p):
    part = lambda i: slice(128 * i, 128 * i + 128)
    eliminate(ref, 128 * p)
    inner = ref[part(p), part(p)]
    others = [(p + 1) % 3, (p + 2) % 3]
    for j in others:
        ref[part(p), part(j)] = dot(inner, ref[part(p), part(j)])
    for i in others:
        left = ref[part(i), part(p)]
        for j in others:
            ref[part(i), part(j)] -= dot(left, ref[part(p), part(j)])
        ref[part(i), part(p)] = -dot(left, inner)


def kernel(
    x_ref, val_ref, var_ref, rows_ref, owner_ref, out_ref,
    oa_ref, gram_ref, cross_ref, s1, s2, ut_ref, f_ref,
    t_in, t_z, t_y, t_s, l_src, l_in, l_mine, l_all, anom,
    g_part, g_one, g_red, g_two, c_part, c_one, c_red, c_two, c_sum,
    t_send, t_recv, l_send, l_recv, g_send, g_recv, x_send, x_recv, c_send, c_recv,
):
    s = lax.axis_index("state")
    m = lax.axis_index("member")
    z, y = lax.div(m, SIDE), lax.rem(m, SIDE)
    xpos, core = lax.div(s, 2), lax.rem(s, 2)

    def hop(v, k):
        return lax.rem(v + k, SIDE)

    def peer(axis, k):
        if axis == "z":
            return (s, hop(z, k) * SIDE + y)
        if axis == "y":
            return (s, z * SIDE + hop(y, k))
        return (hop(s, k), m)

    barrier = pltpu.get_barrier_semaphore()
    for axis in ("z", "y", "s"):
        for k in range(1, SIDE):
            pl.semaphore_signal(barrier, inc=1, device_id=peer(axis, k), device_id_type=MESH)

    def copy(src, dst, send, recv, where):
        c = pltpu.make_async_remote_copy(
            src_ref=src, dst_ref=dst, send_sem=send, recv_sem=recv, device_id=where, device_id_type=MESH
        )
        c.start()
        return c

    def arrive(copies):
        for c in copies:
            c.wait_recv()

    started = []

    def fan(axis, src, dst, send, recv):
        out = [copy(src(k), dst(k), send.at[k], recv.at[k], peer(axis, k)) for k in range(1, SIDE)]
        started.extend(out)
        return out

    x = x_ref[...]
    spot = lax.broadcasted_iota(jnp.int32, (ROWS, 128), 0)
    picked = []
    for b in range(6):
        lanes = slice(128 * (b % 3), 128 * (b % 3) + 128)
        held = owner_ref[b // 3 : b // 3 + 1, b % 3 : b % 3 + 1] == s
        want = jnp.where(held, rows_ref[b // 3 : b // 3 + 1, lanes], -1)
        picked.append(dot(x, jnp.where(spot == want, 1.0, 0.0)))
    lrows = jnp.concatenate(picked, axis=1)
    t_in[...] = jnp.zeros_like(t_in)
    sx = jnp.sum(x, axis=0, keepdims=True)
    sl = jnp.sum(lrows, axis=0, keepdims=True)
    for b in range(5):
        t_in[8 + b : 9 + b, :] = sx[:, 128 * b : 128 * b + 128]
    for b in range(6):
        t_in[b : b + 1, :] = sl[:, 128 * b : 128 * b + 128]
        l_src[4 * b : 4 * b + 4] = lrows[:, 128 * b : 128 * b + 128].reshape(4, 8, 128)
    pl.semaphore_wait(barrier, 3 * (SIDE - 1))

    tz = fan("z", lambda k: t_in, lambda k: t_z.at[k], t_send.at[0], t_recv.at[0])
    ls = fan("s", lambda k: l_src.at[pl.ds(3 * hop(s, k), 3)], lambda k: l_in.at[k], l_send.at[0], l_recv.at[0])
    arrive(ls)
    l_mine[...] = total(l_in, l_src[pl.ds(3 * s, 3)])
    l_all[pl.ds(3 * s, 3)] = l_mine[...]
    la = fan("s", lambda k: l_mine, lambda k: l_all.at[pl.ds(3 * s, 3)], l_send.at[1], l_recv.at[1])
    arrive(tz)
    t_y[0] = total(t_z, t_in[...])
    ty = fan("y", lambda k: t_y.at[0], lambda k: t_y.at[k], t_send.at[1], t_recv.at[1])
    arrive(ty)
    sums = total(t_y, t_y[0])
    t_s[0] = sums[0:8]
    ts = fan("s", lambda k: t_s.at[0], lambda k: t_s.at[k], t_send.at[2], t_recv.at[2])
    xmean = sums[8:16] / MEMBERS
    for b in range(5):
        anom[:, 128 * b : 128 * b + 128] = x[:, 128 * b : 128 * b + 128] - xmean[b : b + 1]
    arrive(la)
    arrive(ts)
    omean = total(t_s, t_s[0]) / MEMBERS
    for b in range(6):
        oa_ref[:, 128 * b : 128 * b + 128] = l_all[4 * b : 4 * b + 4].reshape(MINE, 128) - omean[b : b + 1]

    for i in range(6):
        band = dot(oa_ref[:, 128 * i : 128 * i + 128], oa_ref[:, 0 : 128 * i + 128], (0, 0))
        for j in range(i + 1):
            at = 16 * BLOCKS.index((i, j))
            g_part[at : at + 16] = band[:, 128 * j : 128 * j + 128].reshape(16, 8, 128)
    g_part[336:384] = jnp.zeros((48, 8, 128), F32)

    gbase = s * 48
    order = (("z", z, "y", y), ("y", y, "z", z))
    g1 = []
    for h, (first, a, second, b) in enumerate(order):
        g1.append(
            fan(
                first,
                lambda k: g_part.at[pl.ds(gbase + 24 * h + 3 * hop(a, k), 3)],
                lambda k: g_one.at[h, k],
                g_send.at[h, 0],
                g_recv.at[h, 0],
            )
        )
    for i in range(6):
        band = dot(oa_ref[:, 128 * i : 128 * i + 128], anom[...], (0, 0))
        for j in range(5):
            at = 96 * j + 16 * i
            c_part[at : at + 16] = band[:, 128 * j : 128 * j + 128].reshape(16, 8, 128)
    c_part[480:512] = jnp.zeros((32, 8, 128), F32)

    g2 = []
    for h, (first, a, second, b) in enumerate(order):
        arrive(g1[h])
        g_two[h, 0] = total(g_one.at[h], g_part[pl.ds(gbase + 24 * h + 3 * a, 3)])
        g2.append(
            fan(second, lambda k: g_two.at[h, 0], lambda k: g_two.at[h, k], g_send.at[h, 1], g_recv.at[h, 1])
        )
    g3 = []
    for h, (first, a, second, b) in enumerate(order):
        arrive(g2[h])
        g_red[h] = total(g_two.at[h], g_two[h, 0])
        spot = pl.ds(gbase + 24 * h + 3 * a, 3)
        gram_ref[spot] = g_red[h]
        g3.append(
            fan(first, lambda k: g_red.at[h], lambda k: gram_ref.at[spot], g_send.at[h, 2], g_recv.at[h, 2])
        )
    arrive(g3[0])
    arrive(g3[1])
    mine = pl.ds(gbase, 48)
    gx = []
    for k in range(1, 4):
        where = (lax.rem(xpos + k, 4) * 2 + core, m)
        gx.append(copy(gram_ref.at[mine], gram_ref.at[mine], x_send.at[k], x_recv.at[k], where))
    started.extend(gx)

    def first_step():
        return [
            fan(
                first,
                lambda k: c_part.at[pl.ds(256 * h + 32 * hop(a, k), 32)],
                lambda k: c_one.at[h, k],
                c_send.at[h, 0],
                c_recv.at[h, 0],
            )
            for h, (first, a, second, b) in enumerate(order)
        ]

    def second_step(before):
        out = []
        for h, (first, a, second, b) in enumerate(order):
            arrive(before[h])
            c_red[h] = total(c_one.at[h], c_part[pl.ds(256 * h + 32 * a, 32)])
            out.append(
                fan(
                    second,
                    lambda k: c_red.at[h, pl.ds(4 * hop(b, k), 4)],
                    lambda k: c_two.at[h, k],
                    c_send.at[h, 1],
                    c_recv.at[h, 1],
                )
            )
        return out

    def third_step(before):
        out = []
        for h, (first, a, second, b) in enumerate(order):
            arrive(before[h])
            c_two[h, 0] = total(c_two.at[h], c_red[h, pl.ds(4 * b, 4)])
            spot = pl.ds(4 * b, 4)
            c_sum[h, spot] = c_two[h, 0]
            out.append(
                fan(second, lambda k: c_two.at[h, 0], lambda k: c_sum.at[h, spot], c_send.at[h, 2], c_recv.at[h, 2])
            )
        return out

    def fourth_step(before):
        out = []
        for h, (first, a, second, b) in enumerate(order):
            arrive(before[h])
            spot = pl.ds(256 * h + 32 * a, 32)
            cross_ref[spot] = c_sum[h]
            out.append(
                fan(first, lambda k: c_sum.at[h], lambda k: cross_ref.at[spot], c_send.at[h, 3], c_recv.at[h, 3])
            )
        return out

    steps = first_step()
    gc = []
    for k in range(4):
        if k > 0:
            gx[k - 1].wait_recv()
        got = pl.ds((lax.rem(xpos + 4 - k, 4) * 2 + core) * 48, 48)
        gc.append(copy(gram_ref.at[got], gram_ref.at[got], x_send.at[4 + k], x_recv.at[4 + k], (s + 1 - 2 * core, m)))
    started.extend(gc)
    arrive(gc)

    scale = 1.0 / (MEMBERS - 1.0)
    part = lambda i: slice(128 * i, 128 * i + 128)
    diag = lax.broadcasted_iota(jnp.int32, (128, 128), 0) == lax.broadcasted_iota(jnp.int32, (128, 128), 1)

    def gram(i, j):
        at = 16 * BLOCKS.index((i, j))
        return gram_ref[at : at + 16].reshape(128, 128) * scale

    for i in range(3):
        s1[part(i), part(i)] = gram(i, i) + jnp.where(diag, var_ref[0:1, part(i)], 0.0)
        for j in range(i):
            block = gram(i, j)
            s1[part(i), part(j)] = block
            s1[part(j), part(i)] = block.T
    sweep(s1, 0)
    sweep(s1, 1)
    sweep(s1, 2)
    steps = second_step(steps)
    for i in range(3):
        for j in range(3):
            f_ref[part(i), part(j)] = gram(3 + i, j)
    ut_ref[...] = dot(f_ref[...], s1[...])
    f_ref[...] = 0.75 * f_ref[...] + (0.25 * var_ref[0:1, :]) * ut_ref[...]
    steps = third_step(steps)
    for i in range(3):
        taken = dot(f_ref[part(i), :], ut_ref[0 : 128 * i + 128, :], (1, 1))
        for j in range(i + 1):
            block = gram(3 + i, 3 + j) - taken[:, part(j)]
            if i == j:
                s2[part(i), part(i)] = block + jnp.where(diag, var_ref[1:2, part(i)], 0.0)
            else:
                s2[part(i), part(j)] = block
                s2[part(j), part(i)] = block.T
    sweep(s2, 0)
    steps = fourth_step(steps)
    sweep(s2, 1)
    sweep(s2, 2)
    flat = jnp.concatenate([omean[b : b + 1] for b in range(6)], axis=1)
    gap1, gap2 = val_ref[0:1] - flat[:, :OBS], val_ref[1:2] - flat[:, OBS:]
    o1, o2 = oa_ref[:, :OBS], oa_ref[:, OBS:]
    b1 = gap1 - 0.5 * o1
    b2 = gap2 - 0.5 * o2 - dot(gap1 - 0.25 * o1, ut_ref[...], (1, 1))
    q2 = dot(b2, s2[...])
    q1 = dot(b1 - dot(q2, f_ref[...]), s1[...])
    q = jnp.concatenate([q1, q2], axis=1) * scale
    arrive(steps[0])
    arrive(steps[1])
    for j in range(5):
        out_ref[:, part(j)] = x_ref[:, part(j)] + dot(q, cross_ref[96 * j : 96 * j + 96].reshape(ALL, 128))
    for c in started:
        c.wait_send()


def shards(state, obs_values, noise_var, obs_rows, owner):
    dma = pltpu.SemaphoreType.DMA
    plane = lambda rows, cols: pltpu.VMEM((rows, cols), F32)
    tiles = lambda *lead: pltpu.VMEM((*lead, 8, 128), F32)
    return pl.pallas_call(
        kernel,
        out_shape=jax.ShapeDtypeStruct((MINE, ROWS), F32),
        in_specs=[pl.BlockSpec(memory_space=pltpu.VMEM)] * 5,
        out_specs=pl.BlockSpec(memory_space=pltpu.VMEM),
        scratch_shapes=[
            plane(MINE, ALL), tiles(384), tiles(512), plane(OBS, OBS), plane(OBS, OBS), plane(OBS, OBS), plane(OBS, OBS),
            pltpu.VMEM((16, 128), F32), pltpu.VMEM((SIDE, 16, 128), F32), pltpu.VMEM((SIDE, 16, 128), F32), tiles(SIDE),
            tiles(24), tiles(SIDE, 3), tiles(3), tiles(24), plane(MINE, ROWS),
            tiles(384), tiles(2, SIDE, 3), tiles(2, 3), tiles(2, SIDE, 3),
            tiles(512), tiles(2, SIDE, 32), tiles(2, 32), tiles(2, SIDE, 4), tiles(2, 32),
            dma((3, SIDE)), dma((3, SIDE)), dma((2, SIDE)), dma((2, SIDE)), dma((2, 3, SIDE)), dma((2, 3, SIDE)),
            dma((SIDE,)), dma((SIDE,)), dma((2, 4, SIDE)), dma((2, 4, SIDE)),
        ],
        compiler_params=pltpu.CompilerParams(
            collective_id=0, has_side_effects=True, vmem_limit_bytes=40 * 2**20
        ),
    )(state, obs_values, noise_var, obs_rows, owner)


def solution(mesh):
    placed = (P("member", "state"), P(), P(), P(), P())
    return jax.shard_map(
        shards, mesh=mesh, in_specs=placed, out_specs=P("member", "state"), check_vma=False
    )
```

```python
import functools

import jax
import jax.numpy as jnp
from jax import lax
from jax.experimental import pallas as pl
from jax.experimental.pallas import tpu as pltpu
from jax.sharding import PartitionSpec as P

MESH = pl.DeviceIdType.MESH
F32 = jnp.float32
HIGHEST = lax.Precision.HIGHEST
SIDE = 8
OBS = 384
ALL = 2 * OBS
ROWS = 640
MINE = 32
MEMBERS = 2048
GROUP = MINE * SIDE
BLOCKS = [(i, j) for i in range(6) for j in range(i + 1)]
HALVES = (0, 1)


def dot(a, b, over=(1, 0)):
    return lax.dot_general(
        a, b, (((over[0],), (over[1],)), ((), ())), precision=HIGHEST, preferred_element_type=F32
    )


def total(slots, own):
    out = own
    for k in range(1, SIDE):
        out = out + slots[k]
    return out


def eliminate(ref, at):
    spread = functools.partial(jnp.broadcast_to, shape=(8, 128))
    lane = lax.broadcasted_iota(jnp.int32, (8, 128), 1)
    sub = lax.broadcasted_iota(jnp.int32, (8, 128), 0)
    a = [ref[at + 8 * i : at + 8 * i + 8, at : at + 128] for i in range(16)]
    for p in range(16):
        rows = a[p]
        cols = [spread(rows[:, 8 * p + j : 8 * p + j + 1]) for j in range(8)]
        for k in range(8):
            col = cols[k]
            pivot = 1.0 / spread(col[k : k + 1])
            rows = jnp.where(lane == 8 * p + k, jnp.where(sub == k, 1.0, 0.0), rows)
            times = jnp.where(sub == k, 1.0 - pivot, col * pivot)
            for j in range(k + 1, 8):
                cols[j] = cols[j] - times * spread(cols[j][k : k + 1])
            rows = rows - times * spread(rows[k : k + 1])
        each = [spread(rows[j : j + 1]) for j in range(8)]
        inside = (lane >= 8 * p) & (lane < 8 * p + 8)
        for i in [(p + 1 + i) % 16 for i in range(15)]:
            old = a[i]
            t = [spread(old[:, 8 * p + j : 8 * p + j + 1]) * each[j] for j in range(8)]
            low, high = (t[0] + t[1]) + (t[2] + t[3]), (t[4] + t[5]) + (t[6] + t[7])
            a[i] = jnp.where(inside, 0.0, old) - (low + high)
        a[p] = rows
    for i in range(16):
        ref[at + 8 * i : at + 8 * i + 8, at : at + 128] = a[i]


def sweep(ref, p):
    part = lambda i: slice(128 * i, 128 * i + 128)
    eliminate(ref, 128 * p)
    inner = ref[part(p), part(p)]
    others = [(p + 1) % 3, (p + 2) % 3]
    for j in others:
        ref[part(p), part(j)] = dot(inner, ref[part(p), part(j)])
    for i in others:
        left = ref[part(i), part(p)]
        for j in others:
            ref[part(i), part(j)] -= dot(left, ref[part(p), part(j)])
        ref[part(i), part(p)] = -dot(left, inner)


def kernel(
    x_hbm, val_hbm, var_hbm, rows_hbm, owner_hbm, out_hbm,
    x_ref, val_ref, var_ref, rows_ref, owner_ref, out_ref,
    oa_ref, anom, s1, s2, ut_ref, f_ref, extra,
    t_in, t_z, t_y, t_s, t_all, l_src, l_in, l_mine, l_all,
    p_part, p_one, p_two, p_red, p_sum, r_part, r_one, r_two, r_red, r_sum,
    c_part, c_one, c_red, c_two, c_sum, cross_ref,
    in_sem, t_send, t_recv, l_send, l_recv, p_send, p_recv, r_send, r_recv, x_send, x_recv, c_send, c_recv,
):
    s = lax.axis_index("state")
    m = lax.axis_index("member")
    z, y = lax.div(m, SIDE), lax.rem(m, SIDE)
    xpos, core = lax.div(s, 2), lax.rem(s, 2)

    def hop(v, k):
        return lax.rem(v + k, SIDE)

    def peer(axis, k):
        if axis == "z":
            return (s, hop(z, k) * SIDE + y)
        if axis == "y":
            return (s, z * SIDE + hop(y, k))
        return (hop(s, k), m)

    loads = []
    pairs = ((x_hbm, x_ref), (rows_hbm, rows_ref), (owner_hbm, owner_ref), (val_hbm, val_ref), (var_hbm, var_ref))
    for i, (src, dst) in enumerate(pairs):
        c = pltpu.make_async_copy(src, dst, in_sem.at[i])
        c.start()
        loads.append(c)
    barrier = pltpu.get_barrier_semaphore()
    for axis in ("z", "y", "s"):
        for k in range(1, SIDE):
            pl.semaphore_signal(barrier, inc=1, device_id=peer(axis, k), device_id_type=MESH)

    started = []

    def copy(src, dst, send, recv, where):
        c = pltpu.make_async_remote_copy(
            src_ref=src, dst_ref=dst, send_sem=send, recv_sem=recv, device_id=where, device_id_type=MESH
        )
        c.start()
        started.append(c)
        return c

    def arrive(copies):
        for c in copies:
            c.wait_recv()

    def fan(axis, src, dst, send, recv, over=range(1, SIDE)):
        return [copy(src(k), dst(k), send.at[k], recv.at[k], peer(axis, k)) for k in over]

    for c in loads:
        c.wait()
    x = x_ref[...]
    iota = lax.broadcasted_iota(jnp.int32, (ROWS, 128), 0)
    t_in[...] = jnp.zeros_like(t_in)
    for b in range(6):
        lanes = slice(128 * (b % 3), 128 * (b % 3) + 128)
        held = owner_ref[b // 3 : b // 3 + 1, b % 3 : b % 3 + 1] == s
        want = jnp.where(held, rows_ref[b // 3 : b // 3 + 1, lanes], -1)
        rows = dot(x, jnp.where(iota == want, 1.0, 0.0))
        t_in[b : b + 1, :] = jnp.sum(rows, axis=0, keepdims=True)
        l_src[4 * b : 4 * b + 4] = rows.reshape(4, 8, 128)
    sx = jnp.sum(x, axis=0, keepdims=True)
    for b in range(5):
        t_in[8 + b : 9 + b, :] = sx[:, 128 * b : 128 * b + 128]
    pl.semaphore_wait(barrier, 3 * (SIDE - 1))

    tz = fan("z", lambda k: t_in, lambda k: t_z.at[k], t_send.at[0], t_recv.at[0])
    ls = fan("s", lambda k: l_src.at[pl.ds(3 * hop(s, k), 3)], lambda k: l_in.at[k], l_send.at[0], l_recv.at[0])
    arrive(ls)
    l_mine[...] = total(l_in, l_src[pl.ds(3 * s, 3)])
    l_all[pl.ds(3 * s, 3)] = l_mine[...]
    la = fan("s", lambda k: l_mine, lambda k: l_all.at[pl.ds(3 * s, 3)], l_send.at[1], l_recv.at[1])
    arrive(tz)
    t_y[0] = total(t_z, t_in[...])
    ts = fan("s", lambda k: t_y.at[0, 0:8], lambda k: t_s.at[k], t_send.at[1], t_recv.at[1])
    ty = fan("y", lambda k: t_y.at[0], lambda k: t_y.at[k], t_send.at[2], t_recv.at[2])
    xnear = t_y[0, 8:16] * (1.0 / GROUP)
    for b in range(5):
        anom[:, 128 * b : 128 * b + 128] = x[:, 128 * b : 128 * b + 128] - xnear[b : b + 1]
    arrive(la)
    arrive(ts)
    onear = total(t_s, t_y[0, 0:8]) * (1.0 / GROUP)
    for b in range(6):
        oa_ref[:, 128 * b : 128 * b + 128] = l_all[4 * b : 4 * b + 4].reshape(MINE, 128) - onear[b : b + 1]

    order = (("z", z, "y", y), ("y", y, "z", z))

    class Gram:
        def __init__(self, n, part, one, two, red, out, send, recv, at):
            self.n, self.part, self.one, self.two, self.red, self.out = n, part, one, two, red, out
            self.send, self.recv, self.at = send, recv, at
            self.base = s * (16 * n)

        def piece(self, h, place):
            return pl.ds(self.base + 8 * self.n * h + self.n * place, self.n)

        def scatter(self):
            self.now = [
                fan(
                    order[h][0],
                    lambda k: self.part.at[self.piece(h, hop(order[h][1], k))],
                    lambda k: self.one.at[h, k],
                    self.send.at[h, 0],
                    self.recv.at[h, 0],
                )
                for h in HALVES
            ]

        def exchange(self):
            after = []
            for h in HALVES:
                arrive(self.now[h])
                self.two[h, 0] = total(self.one.at[h], self.part[self.piece(h, order[h][1])])
                after.append(
                    fan(
                        order[h][2],
                        lambda k: self.two.at[h, 0],
                        lambda k: self.two.at[h, k],
                        self.send.at[h, 1],
                        self.recv.at[h, 1],
                    )
                )
            self.now = after

        def gather(self):
            after = []
            for h in HALVES:
                arrive(self.now[h])
                self.red[h] = total(self.two.at[h], self.two[h, 0])
                piece = self.piece(h, order[h][1])
                self.out[piece] = self.red[h]
                after.append(
                    fan(
                        order[h][0],
                        lambda k: self.red.at[h],
                        lambda k: self.out.at[piece],
                        self.send.at[h, 2],
                        self.recv.at[h, 2],
                    )
                )
            self.now = after

        def spread_chips(self):
            arrive(self.now[0] + self.now[1])
            mine = self.out.at[pl.ds(self.base, 16 * self.n)]
            self.now = [
                copy(mine, mine, x_send.at[self.at, k], x_recv.at[self.at, k], (lax.rem(xpos + k, 4) * 2 + core, m))
                for k in range(1, 4)
            ]

        def spread_cores(self):
            after = []
            for k in range(4):
                if k > 0:
                    self.now[k - 1].wait_recv()
                got = self.out.at[pl.ds((lax.rem(xpos + 4 - k, 4) * 2 + core) * (16 * self.n), 16 * self.n)]
                after.append(
                    copy(got, got, x_send.at[self.at, 4 + k], x_recv.at[self.at, 4 + k], (s + 1 - 2 * core, m))
                )
            self.now = after

        def finish(self):
            arrive(self.now)

    first = Gram(1, p_part, p_one, p_two, p_red, p_sum, p_send, p_recv, 0)
    rest = Gram(2, r_part, r_one, r_two, r_red, r_sum, r_send, r_recv, 1)

    def bands(which, into, skip):
        for i in which:
            band = dot(oa_ref[:, 128 * i : 128 * i + 128], oa_ref[:, 0 : 128 * i + 128], (0, 0))
            for j in range(i + 1):
                at = 16 * (BLOCKS.index((i, j)) - skip)
                into[at : at + 16] = band[:, 128 * j : 128 * j + 128].reshape(16, 8, 128)

    bands(range(3), p_part, 0)
    p_part[96:128] = jnp.zeros((32, 8, 128), F32)
    first.scatter()
    bands(range(3, 6), r_part, 6)
    r_part[240:256] = jnp.zeros((16, 8, 128), F32)
    for i in range(6):
        band = dot(oa_ref[:, 128 * i : 128 * i + 128], anom[...], (0, 0))
        for j in range(5):
            at = 96 * j + 16 * i
            c_part[at : at + 16] = band[:, 128 * j : 128 * j + 128].reshape(16, 8, 128)
    c_part[480:512] = jnp.zeros((32, 8, 128), F32)

    cross_steps = [[], []]

    def cross_scatter(over):
        for h in HALVES:
            cross_steps[h] += fan(
                order[h][0],
                lambda k: c_part.at[pl.ds(256 * h + 32 * hop(order[h][1], k), 32)],
                lambda k: c_one.at[h, k],
                c_send.at[h, 0],
                c_recv.at[h, 0],
                over,
            )

    def cross_second():
        for h in HALVES:
            arrive(cross_steps[h])
            c_red[h] = total(c_one.at[h], c_part[pl.ds(256 * h + 32 * order[h][1], 32)])
            cross_steps[h] = fan(
                order[h][2],
                lambda k: c_red.at[h, pl.ds(4 * hop(order[h][3], k), 4)],
                lambda k: c_two.at[h, k],
                c_send.at[h, 1],
                c_recv.at[h, 1],
            )

    def cross_third():
        for h in HALVES:
            arrive(cross_steps[h])
            spot = pl.ds(4 * order[h][3], 4)
            c_two[h, 0] = total(c_two.at[h], c_red[h, spot])
            c_sum[h, spot] = c_two[h, 0]
            cross_steps[h] = fan(
                order[h][2], lambda k: c_two.at[h, 0], lambda k: c_sum.at[h, spot], c_send.at[h, 2], c_recv.at[h, 2]
            )

    def cross_fourth():
        for h in HALVES:
            arrive(cross_steps[h])
            spot = pl.ds(256 * h + 32 * order[h][1], 32)
            cross_ref[spot] = c_sum[h]
            cross_steps[h] = fan(
                order[h][0], lambda k: c_sum.at[h], lambda k: cross_ref.at[spot], c_send.at[h, 3], c_recv.at[h, 3]
            )

    cross_scatter((1, 7))
    first.exchange()
    rest.scatter()
    arrive(ty)
    ta = fan("s", lambda k: t_y.at[:, 0:8], lambda k: t_all.at[k], t_send.at[3], t_recv.at[3])
    cross_scatter((2, 6))
    first.gather()
    rest.exchange()
    cross_scatter((3, 5))

    arrive(ta)
    obs_means = total(t_all, t_y[:, 0:8]) * (1.0 / GROUP)
    flat = jnp.concatenate([obs_means[:, b, :] for b in range(6)], axis=1)
    near = flat[0:1]
    omean = jnp.mean(flat, axis=0, keepdims=True)
    apart = flat - omean
    row_means = jnp.concatenate([t_y[:, 8 + b, :] for b in range(5)], axis=1) * (1.0 / GROUP)
    row_apart = row_means - jnp.mean(row_means, axis=0, keepdims=True)
    for i in range(6):
        band = dot(apart[:, 128 * i : 128 * i + 128] * float(GROUP), apart[:, 0 : 128 * i + 128], (0, 0))
        for j in range(i + 1):
            at = 16 * BLOCKS.index((i, j))
            extra[at : at + 16] = band[:, 128 * j : 128 * j + 128].reshape(16, 8, 128)

    first.spread_chips()
    rest.gather()
    cross_scatter((4,))
    first.spread_cores()
    first.finish()

    scale = 1.0 / (MEMBERS - 1.0)
    part = lambda i: slice(128 * i, 128 * i + 128)
    diag = lax.broadcasted_iota(jnp.int32, (128, 128), 0) == lax.broadcasted_iota(jnp.int32, (128, 128), 1)

    def gram(i, j):
        at = 16 * BLOCKS.index((i, j))
        tiles = p_sum[at : at + 16] if at < 96 else r_sum[at - 96 : at - 80]
        return ((tiles + extra[at : at + 16]) * scale).reshape(128, 128)

    for i in range(3):
        s1[part(i), part(i)] = gram(i, i) + jnp.where(diag, var_ref[0:1, part(i)], 0.0)
        for j in range(i):
            block = gram(i, j)
            s1[part(i), part(j)] = block
            s1[part(j), part(i)] = block.T
    rest.spread_chips()
    sweep(s1, 0)
    cross_second()
    rest.spread_cores()
    sweep(s1, 1)
    cross_third()
    sweep(s1, 2)
    cross_fourth()
    rest.finish()
    for i in range(3):
        for j in range(3):
            f_ref[part(i), part(j)] = gram(3 + i, j)
    ut_ref[...] = dot(f_ref[...], s1[...])
    f_ref[...] = 0.75 * f_ref[...] + (0.25 * var_ref[0:1, :]) * ut_ref[...]
    for i in range(3):
        taken = dot(f_ref[part(i), :], ut_ref[0 : 128 * i + 128, :], (1, 1))
        for j in range(i + 1):
            block = gram(3 + i, 3 + j) - taken[:, part(j)]
            if i == j:
                s2[part(i), part(i)] = block + jnp.where(diag, var_ref[1:2, part(i)], 0.0)
            else:
                s2[part(i), part(j)] = block
                s2[part(j), part(i)] = block.T
    for p in range(3):
        sweep(s2, p)
    gap = jnp.concatenate([val_ref[0:1], val_ref[1:2]], axis=1) - omean
    about = oa_ref[...] + (near - omean)
    gap1, gap2, o1, o2 = gap[:, :OBS], gap[:, OBS:], about[:, :OBS], about[:, OBS:]
    b1 = gap1 - 0.5 * o1
    b2 = gap2 - 0.5 * o2 - dot(gap1 - 0.25 * o1, ut_ref[...], (1, 1))
    q2 = dot(b2, s2[...])
    q1 = dot(b1 - dot(q2, f_ref[...]), s1[...])
    q = jnp.concatenate([q1, q2], axis=1) * scale
    low = dot(q, apart, (1, 1)) * float(GROUP)
    arrive(cross_steps[0] + cross_steps[1])
    for j in range(5):
        block = cross_ref[96 * j : 96 * j + 96].reshape(ALL, 128)
        out_ref[:, part(j)] = x_ref[:, part(j)] + (dot(q, block) + dot(low, row_apart[:, part(j)]))
    done = pltpu.make_async_copy(out_ref, out_hbm, in_sem.at[5])
    done.start()
    for c in started:
        c.wait_send()
    done.wait()


def shards(state, obs_values, noise_var, obs_rows, owner):
    dma = pltpu.SemaphoreType.DMA
    plane = lambda rows, cols: pltpu.VMEM((rows, cols), F32)
    tiles = lambda *lead: pltpu.VMEM((*lead, 8, 128), F32)
    return pl.pallas_call(
        kernel,
        out_shape=jax.ShapeDtypeStruct((MINE, ROWS), F32),
        in_specs=[pl.BlockSpec(memory_space=pl.ANY)] * 5,
        out_specs=pl.BlockSpec(memory_space=pl.ANY),
        scratch_shapes=[
            plane(MINE, ROWS), plane(2, OBS), plane(2, OBS), pltpu.VMEM((2, OBS), jnp.int32), pltpu.VMEM((2, 3), jnp.int32),
            plane(MINE, ROWS),
            plane(MINE, ALL), plane(MINE, ROWS), plane(OBS, OBS), plane(OBS, OBS), plane(OBS, OBS), plane(OBS, OBS), tiles(336),
            plane(16, 128), pltpu.VMEM((SIDE, 16, 128), F32), pltpu.VMEM((SIDE, 16, 128), F32), tiles(SIDE), tiles(SIDE, SIDE),
            tiles(24), tiles(SIDE, 3), tiles(3), tiles(24),
            tiles(128), tiles(2, SIDE, 1), tiles(2, SIDE, 1), tiles(2, 1), tiles(128),
            tiles(256), tiles(2, SIDE, 2), tiles(2, SIDE, 2), tiles(2, 2), tiles(256),
            tiles(512), tiles(2, SIDE, 32), tiles(2, 32), tiles(2, SIDE, 4), tiles(2, 32), tiles(512),
            dma((6,)), dma((4, SIDE)), dma((4, SIDE)), dma((2, SIDE)), dma((2, SIDE)),
            dma((2, 3, SIDE)), dma((2, 3, SIDE)), dma((2, 3, SIDE)), dma((2, 3, SIDE)),
            dma((2, SIDE)), dma((2, SIDE)), dma((2, 4, SIDE)), dma((2, 4, SIDE)),
        ],
        compiler_params=pltpu.CompilerParams(
            collective_id=0, has_side_effects=True, vmem_limit_bytes=60 * 2**20
        ),
    )(state, obs_values, noise_var, obs_rows, owner)


def solution(mesh):
    placed = (P("member", "state"), P(), P(), P(), P())
    return jax.shard_map(
        shards, mesh=mesh, in_specs=placed, out_specs=P("member", "state"), check_vma=False
    )
```

```python
import functools

import jax
import jax.numpy as jnp
from jax import lax
from jax.experimental import pallas as pl
from jax.experimental.pallas import tpu as pltpu
from jax.sharding import PartitionSpec as P

MESH = pl.DeviceIdType.MESH
F32 = jnp.float32
HIGHEST = lax.Precision.HIGHEST
SIDE = 8
OBS = 384
ALL = 2 * OBS
ROWS = 640
MINE = 32
MEMBERS = 2048
GROUP = MINE * SIDE
SHARE = ROWS // SIDE
BLOCKS = [(i, j) for i in range(6) for j in range(i + 1)]
HALVES = (0, 1)


def dot(a, b, over=(1, 0)):
    return lax.dot_general(
        a, b, (((over[0],), (over[1],)), ((), ())), precision=HIGHEST, preferred_element_type=F32
    )


def total(slots, own):
    out = own
    for k in range(1, SIDE):
        out = out + slots[k]
    return out


def eliminate(ref, at):
    spread = functools.partial(jnp.broadcast_to, shape=(8, 128))
    lane = lax.broadcasted_iota(jnp.int32, (8, 128), 1)
    sub = lax.broadcasted_iota(jnp.int32, (8, 128), 0)
    a = [ref[at + 8 * i : at + 8 * i + 8, at : at + 128] for i in range(16)]
    for p in range(16):
        rows = a[p]
        cols = [spread(rows[:, 8 * p + j : 8 * p + j + 1]) for j in range(8)]
        for k in range(8):
            col = cols[k]
            pivot = 1.0 / spread(col[k : k + 1])
            rows = jnp.where(lane == 8 * p + k, jnp.where(sub == k, 1.0, 0.0), rows)
            times = jnp.where(sub == k, 1.0 - pivot, col * pivot)
            for j in range(k + 1, 8):
                cols[j] = cols[j] - times * spread(cols[j][k : k + 1])
            rows = rows - times * spread(rows[k : k + 1])
        each = [spread(rows[j : j + 1]) for j in range(8)]
        inside = (lane >= 8 * p) & (lane < 8 * p + 8)
        for i in [(p + 1 + i) % 16 for i in range(15)]:
            old = a[i]
            t = [spread(old[:, 8 * p + j : 8 * p + j + 1]) * each[j] for j in range(8)]
            low, high = (t[0] + t[1]) + (t[2] + t[3]), (t[4] + t[5]) + (t[6] + t[7])
            a[i] = jnp.where(inside, 0.0, old) - (low + high)
        a[p] = rows
    for i in range(16):
        ref[at + 8 * i : at + 8 * i + 8, at : at + 128] = a[i]


def sweep(ref, p):
    part = lambda i: slice(128 * i, 128 * i + 128)
    eliminate(ref, 128 * p)
    inner = ref[part(p), part(p)]
    others = [(p + 1) % 3, (p + 2) % 3]
    for j in others:
        ref[part(p), part(j)] = dot(inner, ref[part(p), part(j)])
    for i in others:
        left = ref[part(i), part(p)]
        for j in others:
            ref[part(i), part(j)] -= dot(left, ref[part(p), part(j)])
        ref[part(i), part(p)] = -dot(left, inner)


def kernel(
    x_hbm, val_hbm, var_hbm, rows_hbm, owner_hbm, out_hbm,
    x_ref, val_ref, var_ref, rows_ref, owner_ref, out_ref,
    oa_ref, s1, s2, ut_ref, f_ref, extra,
    t_in, t_z, t_y, t_s, t_all, l_src, l_in, l_mine, l_all,
    p_part, p_one, p_two, p_red, p_sum, r_part, r_one, r_two, r_red, r_sum,
    o_big, o_mat, a_src, a_in, c_part, c_one, c_red, c_sum, d_src, d_in,
    in_sem, t_send, t_recv, l_send, l_recv, p_send, p_recv, r_send, r_recv, x_send, x_recv, o_send, o_recv, c_send, c_recv,
):
    s = lax.axis_index("state")
    m = lax.axis_index("member")
    z, y = lax.div(m, SIDE), lax.rem(m, SIDE)
    xpos, core = lax.div(s, 2), lax.rem(s, 2)

    def hop(v, k):
        return lax.rem(v + k, SIDE)

    def peer(axis, k):
        if axis == "z":
            return (s, hop(z, k) * SIDE + y)
        if axis == "y":
            return (s, z * SIDE + hop(y, k))
        return (hop(s, k), m)

    loads = []
    pairs = ((x_hbm, x_ref), (rows_hbm, rows_ref), (owner_hbm, owner_ref), (val_hbm, val_ref), (var_hbm, var_ref))
    for i, (src, dst) in enumerate(pairs):
        c = pltpu.make_async_copy(src, dst, in_sem.at[i])
        c.start()
        loads.append(c)
    barrier = pltpu.get_barrier_semaphore()
    for axis in ("z", "y", "s"):
        for k in range(1, SIDE):
            pl.semaphore_signal(barrier, inc=1, device_id=peer(axis, k), device_id_type=MESH)

    started = []

    def copy(src, dst, send, recv, where):
        c = pltpu.make_async_remote_copy(
            src_ref=src, dst_ref=dst, send_sem=send, recv_sem=recv, device_id=where, device_id_type=MESH
        )
        c.start()
        started.append(c)
        return c

    def arrive(copies):
        for c in copies:
            c.wait_recv()

    def fan(axis, src, dst, send, recv, over=range(1, SIDE)):
        return [copy(src(k), dst(k), send.at[k], recv.at[k], peer(axis, k)) for k in over]

    for c in loads:
        c.wait()
    x = x_ref[...]
    iota = lax.broadcasted_iota(jnp.int32, (ROWS, 128), 0)
    t_in[...] = jnp.zeros_like(t_in)
    for b in range(6):
        lanes = slice(128 * (b % 3), 128 * (b % 3) + 128)
        held = owner_ref[b // 3 : b // 3 + 1, b % 3 : b % 3 + 1] == s
        want = jnp.where(held, rows_ref[b // 3 : b // 3 + 1, lanes], -1)
        rows = dot(x, jnp.where(iota == want, 1.0, 0.0))
        t_in[b : b + 1, :] = jnp.sum(rows, axis=0, keepdims=True)
        l_src[4 * b : 4 * b + 4] = rows.reshape(4, 8, 128)
    sx = jnp.sum(x, axis=0, keepdims=True)
    for b in range(5):
        t_in[8 + b : 9 + b, :] = sx[:, 128 * b : 128 * b + 128]
    pl.semaphore_wait(barrier, 3 * (SIDE - 1))

    tz = fan("z", lambda k: t_in, lambda k: t_z.at[k], t_send.at[0], t_recv.at[0])
    ls = fan("s", lambda k: l_src.at[pl.ds(3 * hop(s, k), 3)], lambda k: l_in.at[k], l_send.at[0], l_recv.at[0])
    arrive(ls)
    l_mine[...] = total(l_in, l_src[pl.ds(3 * s, 3)])
    l_all[pl.ds(3 * s, 3)] = l_mine[...]
    la = fan("s", lambda k: l_mine, lambda k: l_all.at[pl.ds(3 * s, 3)], l_send.at[1], l_recv.at[1])
    mine = pl.ds(3 * s, 3)
    o_big[0, mine] = l_mine[...]
    ya = fan("y", lambda k: l_mine, lambda k: o_big.at[k, mine], o_send.at[0], o_recv.at[0])
    arrive(tz)
    t_y[0] = total(t_z, t_in[...])
    ts = fan("s", lambda k: t_y.at[0, 0:8], lambda k: t_s.at[k], t_send.at[1], t_recv.at[1])
    ty = fan("y", lambda k: t_y.at[0], lambda k: t_y.at[k], t_send.at[2], t_recv.at[2])
    arrive(la)
    arrive(ts)
    onear = total(t_s, t_y[0, 0:8]) * (1.0 / GROUP)
    for b in range(6):
        oa_ref[:, 128 * b : 128 * b + 128] = l_all[4 * b : 4 * b + 4].reshape(MINE, 128) - onear[b : b + 1]

    order = (("z", z, "y", y), ("y", y, "z", z))

    class Gram:
        def __init__(self, n, part, one, two, red, out, send, recv, at):
            self.n, self.part, self.one, self.two, self.red, self.out = n, part, one, two, red, out
            self.send, self.recv, self.at = send, recv, at
            self.base = s * (16 * n)

        def piece(self, h, place):
            return pl.ds(self.base + 8 * self.n * h + self.n * place, self.n)

        def scatter(self):
            self.now = [
                fan(
                    order[h][0],
                    lambda k: self.part.at[self.piece(h, hop(order[h][1], k))],
                    lambda k: self.one.at[h, k],
                    self.send.at[h, 0],
                    self.recv.at[h, 0],
                )
                for h in HALVES
            ]

        def exchange(self):
            after = []
            for h in HALVES:
                arrive(self.now[h])
                self.two[h, 0] = total(self.one.at[h], self.part[self.piece(h, order[h][1])])
                after.append(
                    fan(
                        order[h][2],
                        lambda k: self.two.at[h, 0],
                        lambda k: self.two.at[h, k],
                        self.send.at[h, 1],
                        self.recv.at[h, 1],
                    )
                )
            self.now = after

        def gather(self):
            after = []
            for h in HALVES:
                arrive(self.now[h])
                self.red[h] = total(self.two.at[h], self.two[h, 0])
                piece = self.piece(h, order[h][1])
                self.out[piece] = self.red[h]
                after.append(
                    fan(
                        order[h][0],
                        lambda k: self.red.at[h],
                        lambda k: self.out.at[piece],
                        self.send.at[h, 2],
                        self.recv.at[h, 2],
                    )
                )
            self.now = after

        def spread_chips(self):
            arrive(self.now[0] + self.now[1])
            mine = self.out.at[pl.ds(self.base, 16 * self.n)]
            self.now = [
                copy(mine, mine, x_send.at[self.at, k], x_recv.at[self.at, k], (lax.rem(xpos + k, 4) * 2 + core, m))
                for k in range(1, 4)
            ]

        def spread_cores(self):
            after = []
            for k in range(4):
                if k > 0:
                    self.now[k - 1].wait_recv()
                got = self.out.at[pl.ds((lax.rem(xpos + 4 - k, 4) * 2 + core) * (16 * self.n), 16 * self.n)]
                after.append(
                    copy(got, got, x_send.at[self.at, 4 + k], x_recv.at[self.at, 4 + k], (s + 1 - 2 * core, m))
                )
            self.now = after

        def finish(self):
            arrive(self.now)

    first = Gram(1, p_part, p_one, p_two, p_red, p_sum, p_send, p_recv, 0)
    rest = Gram(2, r_part, r_one, r_two, r_red, r_sum, r_send, r_recv, 1)

    def bands(which, into, skip):
        for i in which:
            band = dot(oa_ref[:, 128 * i : 128 * i + 128], oa_ref[:, 0 : 128 * i + 128], (0, 0))
            for j in range(i + 1):
                at = 16 * (BLOCKS.index((i, j)) - skip)
                into[at : at + 16] = band[:, 128 * j : 128 * j + 128].reshape(16, 8, 128)

    bands(range(3), p_part, 0)
    p_part[96:128] = jnp.zeros((32, 8, 128), F32)
    first.scatter()
    bands(range(3, 6), r_part, 6)
    r_part[240:256] = jnp.zeros((16, 8, 128), F32)
    arrive(ya)
    ox = [
        copy(
            o_big.at[:, mine],
            o_big.at[:, mine],
            o_send.at[1, k],
            o_recv.at[1, k],
            (lax.rem(xpos + k, 4) * 2 + core, m),
        )
        for k in range(1, 4)
    ]
    arrive(ty)
    ta = fan("s", lambda k: t_y.at[:, 0:8], lambda k: t_all.at[k], t_send.at[3], t_recv.at[3])
    row_means = sum(t_y[k, 8:16] for k in range(SIDE)) * (1.0 / MEMBERS)
    about = x - jnp.concatenate([row_means[b : b + 1] for b in range(5)], axis=1)
    a_src[...] = jnp.zeros_like(a_src)
    for c in range(SIDE):
        a_src[c, :, 0:SHARE] = about[:, SHARE * c : SHARE * c + SHARE]
    a_in[0] = a_src[y]
    first.exchange()
    aa = fan("y", lambda k: a_src.at[hop(y, k)], lambda k: a_in.at[k], c_send.at[0], c_recv.at[0])
    rest.scatter()
    oc = []
    for k in range(4):
        if k > 0:
            ox[k - 1].wait_recv()
        got = o_big.at[:, pl.ds(3 * (lax.rem(xpos + 4 - k, 4) * 2 + core), 3)]
        oc.append(copy(got, got, o_send.at[1, 4 + k], o_recv.at[1, 4 + k], (s + 1 - 2 * core, m)))

    arrive(ta)
    obs_means = total(t_all, t_y[:, 0:8]) * (1.0 / GROUP)
    flat = jnp.concatenate([obs_means[:, b, :] for b in range(6)], axis=1)
    omean = jnp.mean(flat, axis=0, keepdims=True)
    apart = flat - omean
    for i in range(6):
        band = dot(apart[:, 128 * i : 128 * i + 128] * float(GROUP), apart[:, 0 : 128 * i + 128], (0, 0))
        for j in range(i + 1):
            at = 16 * BLOCKS.index((i, j))
            extra[at : at + 16] = band[:, 128 * j : 128 * j + 128].reshape(16, 8, 128)

    first.gather()
    rest.exchange()
    arrive(aa + oc)
    for k in range(SIDE):
        for b in range(6):
            lanes = slice(128 * b, 128 * b + 128)
            o_mat[32 * k : 32 * k + 32, lanes] = o_big[k, 4 * b : 4 * b + 4].reshape(MINE, 128) - omean[:, lanes]
    c_part[60:64] = jnp.zeros((4, 8, 128), F32)
    for b in range(6):
        band = dot(a_in[...].reshape(GROUP, 128), o_mat[:, 128 * b : 128 * b + 128], (0, 0))
        c_part[10 * b : 10 * b + 10] = band[0:SHARE].reshape(10, 8, 128)
    first.spread_chips()
    c1 = fan("z", lambda k: c_part.at[pl.ds(8 * hop(z, k), 8)], lambda k: c_one.at[k], c_send.at[1], c_recv.at[1])
    rest.gather()
    first.spread_cores()
    first.finish()

    scale = 1.0 / (MEMBERS - 1.0)
    part = lambda i: slice(128 * i, 128 * i + 128)
    diag = lax.broadcasted_iota(jnp.int32, (128, 128), 0) == lax.broadcasted_iota(jnp.int32, (128, 128), 1)

    def gram(i, j):
        at = 16 * BLOCKS.index((i, j))
        tiles = p_sum[at : at + 16] if at < 96 else r_sum[at - 96 : at - 80]
        return ((tiles + extra[at : at + 16]) * scale).reshape(128, 128)

    for i in range(3):
        s1[part(i), part(i)] = gram(i, i) + jnp.where(diag, var_ref[0:1, part(i)], 0.0)
        for j in range(i):
            block = gram(i, j)
            s1[part(i), part(j)] = block
            s1[part(j), part(i)] = block.T
    rest.spread_chips()
    sweep(s1, 0)
    rest.spread_cores()
    arrive(c1)
    piece = pl.ds(8 * z, 8)
    c_red[...] = total(c_one, c_part[piece])
    c_sum[piece] = c_red[...]
    c2 = fan("z", lambda k: c_red, lambda k: c_sum.at[piece], c_send.at[2], c_recv.at[2])
    sweep(s1, 1)
    sweep(s1, 2)
    rest.finish()
    for i in range(3):
        for j in range(3):
            f_ref[part(i), part(j)] = gram(3 + i, j)
    ut_ref[...] = dot(f_ref[...], s1[...])
    f_ref[...] = 0.75 * f_ref[...] + (0.25 * var_ref[0:1, :]) * ut_ref[...]
    for i in range(3):
        taken = dot(f_ref[part(i), :], ut_ref[0 : 128 * i + 128, :], (1, 1))
        for j in range(i + 1):
            block = gram(3 + i, 3 + j) - taken[:, part(j)]
            if i == j:
                s2[part(i), part(i)] = block + jnp.where(diag, var_ref[1:2, part(i)], 0.0)
            else:
                s2[part(i), part(j)] = block
                s2[part(j), part(i)] = block.T
    for p in range(3):
        sweep(s2, p)
    gap = jnp.concatenate([val_ref[0:1], val_ref[1:2]], axis=1) - omean
    arrive(c2)
    cross = jnp.concatenate([c_sum[10 * b : 10 * b + 10].reshape(SHARE, 128) for b in range(6)], axis=1) * scale
    v1 = dot(cross[:, :OBS], s1[...])
    v2 = dot(cross[:, OBS:] - dot(v1, f_ref[...], (1, 1)), s2[...])
    uv = dot(v2, ut_ref[...])
    shift = dot(jnp.broadcast_to(gap, (8, ALL)), jnp.concatenate([v1 - uv, v2], axis=1), (1, 1))
    spread = dot(o_mat[...], jnp.concatenate([0.5 * v1 - 0.25 * uv, 0.5 * v2], axis=1), (1, 1))
    gain = shift[0:1] - spread
    for k in range(SIDE):
        d_src[k, :, 0:SHARE] = gain[32 * k : 32 * k + 32]
        d_src[k, :, SHARE:128] = jnp.zeros((MINE, 128 - SHARE), F32)
    d_in[y] = d_src[0]
    back = fan("y", lambda k: d_src.at[SIDE - k], lambda k: d_in.at[y], c_send.at[3], c_recv.at[3])
    arrive(back)
    for c in range(SIDE):
        lanes = slice(SHARE * c, SHARE * c + SHARE)
        out_ref[:, lanes] = x_ref[:, lanes] + d_in[c, :, 0:SHARE]
    done = pltpu.make_async_copy(out_ref, out_hbm, in_sem.at[5])
    done.start()
    for c in started:
        c.wait_send()
    done.wait()


def shards(state, obs_values, noise_var, obs_rows, owner):
    dma = pltpu.SemaphoreType.DMA
    plane = lambda rows, cols: pltpu.VMEM((rows, cols), F32)
    tiles = lambda *lead: pltpu.VMEM((*lead, 8, 128), F32)
    return pl.pallas_call(
        kernel,
        out_shape=jax.ShapeDtypeStruct((MINE, ROWS), F32),
        in_specs=[pl.BlockSpec(memory_space=pl.ANY)] * 5,
        out_specs=pl.BlockSpec(memory_space=pl.ANY),
        scratch_shapes=[
            plane(MINE, ROWS), plane(2, OBS), plane(2, OBS), pltpu.VMEM((2, OBS), jnp.int32), pltpu.VMEM((2, 3), jnp.int32),
            plane(MINE, ROWS),
            plane(MINE, ALL), plane(OBS, OBS), plane(OBS, OBS), plane(OBS, OBS), plane(OBS, OBS), tiles(336),
            plane(16, 128), pltpu.VMEM((SIDE, 16, 128), F32), pltpu.VMEM((SIDE, 16, 128), F32), tiles(SIDE), tiles(SIDE, SIDE),
            tiles(24), tiles(SIDE, 3), tiles(3), tiles(24),
            tiles(128), tiles(2, SIDE, 1), tiles(2, SIDE, 1), tiles(2, 1), tiles(128),
            tiles(256), tiles(2, SIDE, 2), tiles(2, SIDE, 2), tiles(2, 2), tiles(256),
            tiles(SIDE, 24), plane(GROUP, ALL), pltpu.VMEM((SIDE, MINE, 128), F32), pltpu.VMEM((SIDE, MINE, 128), F32),
            tiles(64), tiles(SIDE, 8), tiles(8), tiles(64),
            pltpu.VMEM((SIDE, MINE, 128), F32), pltpu.VMEM((SIDE, MINE, 128), F32),
            dma((6,)), dma((4, SIDE)), dma((4, SIDE)), dma((2, SIDE)), dma((2, SIDE)),
            dma((2, 3, SIDE)), dma((2, 3, SIDE)), dma((2, 3, SIDE)), dma((2, 3, SIDE)),
            dma((2, SIDE)), dma((2, SIDE)), dma((2, SIDE)), dma((2, SIDE)), dma((4, SIDE)), dma((4, SIDE)),
        ],
        compiler_params=pltpu.CompilerParams(
            collective_id=0, has_side_effects=True, vmem_limit_bytes=40 * 2**20
        ),
    )(state, obs_values, noise_var, obs_rows, owner)


def solution(mesh):
    placed = (P("member", "state"), P(), P(), P(), P())
    return jax.shard_map(
        shards, mesh=mesh, in_specs=placed, out_specs=P("member", "state"), check_vma=False
    )
```

```python
import functools

import jax
import jax.numpy as jnp
from jax import lax
from jax.experimental import pallas as pl
from jax.experimental.pallas import tpu as pltpu
from jax.sharding import PartitionSpec as P

MESH = pl.DeviceIdType.MESH
F32 = jnp.float32
HIGHEST = lax.Precision.HIGHEST
SIDE = 8
OBS = 384
ALL = 2 * OBS
ROWS = 640
MINE = 32
MEMBERS = 2048
GROUP = MINE * SIDE
SHARE = ROWS // SIDE
BLOCKS = [(i, j) for i in range(6) for j in range(i + 1)]
HALVES = (0, 1)


def dot(a, b, over=(1, 0)):
    return lax.dot_general(
        a, b, (((over[0],), (over[1],)), ((), ())), precision=HIGHEST, preferred_element_type=F32
    )


def total(slots, own):
    out = own
    for k in range(1, SIDE):
        out = out + slots[k]
    return out


def eliminate(ref, at):
    spread = functools.partial(jnp.broadcast_to, shape=(8, 128))
    lane = lax.broadcasted_iota(jnp.int32, (8, 128), 1)
    sub = lax.broadcasted_iota(jnp.int32, (8, 128), 0)
    a = [ref[at + 8 * i : at + 8 * i + 8, at : at + 128] for i in range(16)]
    for p in range(16):
        rows = a[p]
        cols = [spread(rows[:, 8 * p + j : 8 * p + j + 1]) for j in range(8)]
        for k in range(8):
            col = cols[k]
            pivot = 1.0 / spread(col[k : k + 1])
            rows = jnp.where(lane == 8 * p + k, jnp.where(sub == k, 1.0, 0.0), rows)
            times = jnp.where(sub == k, 1.0 - pivot, col * pivot)
            for j in range(k + 1, 8):
                cols[j] = cols[j] - times * spread(cols[j][k : k + 1])
            rows = rows - times * spread(rows[k : k + 1])
        each = [spread(rows[j : j + 1]) for j in range(8)]
        inside = (lane >= 8 * p) & (lane < 8 * p + 8)
        for i in [(p + 1 + i) % 16 for i in range(15)]:
            old = a[i]
            t = [spread(old[:, 8 * p + j : 8 * p + j + 1]) * each[j] for j in range(8)]
            low, high = (t[0] + t[1]) + (t[2] + t[3]), (t[4] + t[5]) + (t[6] + t[7])
            a[i] = jnp.where(inside, 0.0, old) - (low + high)
        a[p] = rows
    for i in range(16):
        ref[at + 8 * i : at + 8 * i + 8, at : at + 128] = a[i]


def sweep(ref, p):
    part = lambda i: slice(128 * i, 128 * i + 128)
    eliminate(ref, 128 * p)
    inner = ref[part(p), part(p)]
    others = [(p + 1) % 3, (p + 2) % 3]
    for j in others:
        ref[part(p), part(j)] = dot(inner, ref[part(p), part(j)])
    for i in others:
        left = ref[part(i), part(p)]
        for j in others:
            ref[part(i), part(j)] -= dot(left, ref[part(p), part(j)])
        ref[part(i), part(p)] = -dot(left, inner)


def kernel(
    x_hbm, val_hbm, var_hbm, rows_hbm, owner_hbm, out_hbm,
    x_ref, val_ref, var_ref, rows_ref, owner_ref, out_ref,
    oa_ref, s1, s2, ut_ref, f_ref, extra,
    t_in, t_z, t_y, t_s, t_all, l_src, l_in, l_mine, l_all,
    p_part, p_one, p_two, p_red, p_sum, r_part, r_one, r_two, r_red, r_sum,
    o_big, o_mat, a_src, a_in, c_part, c_one, c_red, c_sum, d_src, d_in,
    in_sem, t_send, t_recv, l_send, l_recv, p_send, p_recv, r_send, r_recv, x_send, x_recv, o_send, o_recv, c_send, c_recv,
):
    s = lax.axis_index("state")
    m = lax.axis_index("member")
    z, y = lax.div(m, SIDE), lax.rem(m, SIDE)
    xpos, core = lax.div(s, 2), lax.rem(s, 2)

    def hop(v, k):
        return lax.rem(v + k, SIDE)

    def peer(axis, k):
        if axis == "z":
            return (s, hop(z, k) * SIDE + y)
        if axis == "y":
            return (s, z * SIDE + hop(y, k))
        return (hop(s, k), m)

    loads = []
    pairs = ((x_hbm, x_ref), (rows_hbm, rows_ref), (owner_hbm, owner_ref), (val_hbm, val_ref), (var_hbm, var_ref))
    for i, (src, dst) in enumerate(pairs):
        c = pltpu.make_async_copy(src, dst, in_sem.at[i])
        c.start()
        loads.append(c)
    barrier = pltpu.get_barrier_semaphore()
    for axis in ("z", "y", "s"):
        for k in range(1, SIDE):
            pl.semaphore_signal(barrier, inc=1, device_id=peer(axis, k), device_id_type=MESH)

    started = []

    def copy(src, dst, send, recv, where):
        c = pltpu.make_async_remote_copy(
            src_ref=src, dst_ref=dst, send_sem=send, recv_sem=recv, device_id=where, device_id_type=MESH
        )
        c.start()
        started.append(c)
        return c

    def arrive(copies):
        for c in copies:
            c.wait_recv()

    def fan(axis, src, dst, send, recv, over=(4, 3, 5, 2, 6, 1, 7)):
        return [copy(src(k), dst(k), send.at[k], recv.at[k], peer(axis, k)) for k in over]

    for c in loads:
        c.wait()
    x = x_ref[...]
    iota = lax.broadcasted_iota(jnp.int32, (ROWS, 128), 0)
    t_in[...] = jnp.zeros_like(t_in)
    for b in range(6):
        lanes = slice(128 * (b % 3), 128 * (b % 3) + 128)
        held = owner_ref[b // 3 : b // 3 + 1, b % 3 : b % 3 + 1] == s
        want = jnp.where(held, rows_ref[b // 3 : b // 3 + 1, lanes], -1)
        rows = dot(x, jnp.where(iota == want, 1.0, 0.0))
        t_in[b : b + 1, :] = jnp.sum(rows, axis=0, keepdims=True)
        l_src[4 * b : 4 * b + 4] = rows.reshape(4, 8, 128)
    sx = jnp.sum(x, axis=0, keepdims=True)
    for b in range(5):
        t_in[8 + b : 9 + b, :] = sx[:, 128 * b : 128 * b + 128]
    pl.semaphore_wait(barrier, 3 * (SIDE - 1))

    tz = fan("z", lambda k: t_in, lambda k: t_z.at[k], t_send.at[0], t_recv.at[0])
    ls = fan("s", lambda k: l_src.at[pl.ds(3 * hop(s, k), 3)], lambda k: l_in.at[k], l_send.at[0], l_recv.at[0])
    arrive(ls)
    l_mine[...] = total(l_in, l_src[pl.ds(3 * s, 3)])
    l_all[pl.ds(3 * s, 3)] = l_mine[...]
    la = fan("s", lambda k: l_mine, lambda k: l_all.at[pl.ds(3 * s, 3)], l_send.at[1], l_recv.at[1])
    mine = pl.ds(3 * s, 3)
    o_big[0, mine] = l_mine[...]
    ya = fan("y", lambda k: l_mine, lambda k: o_big.at[k, mine], o_send.at[0], o_recv.at[0])
    arrive(tz)
    t_y[0] = total(t_z, t_in[...])
    ts = fan("s", lambda k: t_y.at[0, 0:8], lambda k: t_s.at[k], t_send.at[1], t_recv.at[1])
    ty = fan("y", lambda k: t_y.at[0], lambda k: t_y.at[k], t_send.at[2], t_recv.at[2])
    arrive(la)
    arrive(ts)
    onear = total(t_s, t_y[0, 0:8]) * (1.0 / GROUP)
    for b in range(6):
        oa_ref[:, 128 * b : 128 * b + 128] = l_all[4 * b : 4 * b + 4].reshape(MINE, 128) - onear[b : b + 1]

    order = (("z", z, "y", y), ("y", y, "z", z))

    class Gram:
        def __init__(self, n, part, one, two, red, out, send, recv, at):
            self.n, self.part, self.one, self.two, self.red, self.out = n, part, one, two, red, out
            self.send, self.recv, self.at = send, recv, at
            self.base = s * (16 * n)

        def piece(self, h, place):
            return pl.ds(self.base + 8 * self.n * h + self.n * place, self.n)

        def scatter(self):
            self.now = [
                fan(
                    order[h][0],
                    lambda k: self.part.at[self.piece(h, hop(order[h][1], k))],
                    lambda k: self.one.at[h, k],
                    self.send.at[h, 0],
                    self.recv.at[h, 0],
                )
                for h in HALVES
            ]

        def exchange(self):
            after = []
            for h in HALVES:
                arrive(self.now[h])
                self.two[h, 0] = total(self.one.at[h], self.part[self.piece(h, order[h][1])])
                after.append(
                    fan(
                        order[h][2],
                        lambda k: self.two.at[h, 0],
                        lambda k: self.two.at[h, k],
                        self.send.at[h, 1],
                        self.recv.at[h, 1],
                    )
                )
            self.now = after

        def gather(self):
            after = []
            for h in HALVES:
                arrive(self.now[h])
                self.red[h] = total(self.two.at[h], self.two[h, 0])
                piece = self.piece(h, order[h][1])
                self.out[piece] = self.red[h]
                after.append(
                    fan(
                        order[h][0],
                        lambda k: self.red.at[h],
                        lambda k: self.out.at[piece],
                        self.send.at[h, 2],
                        self.recv.at[h, 2],
                    )
                )
            self.now = after

        def spread_chips(self):
            arrive(self.now[0] + self.now[1])
            mine = self.out.at[pl.ds(self.base, 16 * self.n)]
            self.now = [
                copy(mine, mine, x_send.at[self.at, k], x_recv.at[self.at, k], (lax.rem(xpos + k, 4) * 2 + core, m))
                for k in range(1, 4)
            ]

        def spread_cores(self):
            after = []
            for k in range(4):
                if k > 0:
                    self.now[k - 1].wait_recv()
                got = self.out.at[pl.ds((lax.rem(xpos + 4 - k, 4) * 2 + core) * (16 * self.n), 16 * self.n)]
                after.append(
                    copy(got, got, x_send.at[self.at, 4 + k], x_recv.at[self.at, 4 + k], (s + 1 - 2 * core, m))
                )
            self.now = after

        def finish(self):
            arrive(self.now)

    first = Gram(1, p_part, p_one, p_two, p_red, p_sum, p_send, p_recv, 0)
    rest = Gram(2, r_part, r_one, r_two, r_red, r_sum, r_send, r_recv, 1)

    def bands(which, into, skip):
        for i in which:
            band = dot(oa_ref[:, 128 * i : 128 * i + 128], oa_ref[:, 0 : 128 * i + 128], (0, 0))
            for j in range(i + 1):
                at = 16 * (BLOCKS.index((i, j)) - skip)
                into[at : at + 16] = band[:, 128 * j : 128 * j + 128].reshape(16, 8, 128)

    bands(range(3), p_part, 0)
    p_part[96:128] = jnp.zeros((32, 8, 128), F32)
    first.scatter()
    bands(range(3, 6), r_part, 6)
    r_part[240:256] = jnp.zeros((16, 8, 128), F32)
    arrive(ya)
    ox = [
        copy(
            o_big.at[:, mine],
            o_big.at[:, mine],
            o_send.at[1, k],
            o_recv.at[1, k],
            (lax.rem(xpos + k, 4) * 2 + core, m),
        )
        for k in range(1, 4)
    ]
    arrive(ty)
    ta = fan("s", lambda k: t_y.at[:, 0:8], lambda k: t_all.at[k], t_send.at[3], t_recv.at[3])
    row_means = sum(t_y[k, 8:16] for k in range(SIDE)) * (1.0 / MEMBERS)
    about = x - jnp.concatenate([row_means[b : b + 1] for b in range(5)], axis=1)
    a_src[...] = jnp.zeros_like(a_src)
    for c in range(SIDE):
        a_src[c, :, 0:SHARE] = about[:, SHARE * c : SHARE * c + SHARE]
    a_in[0] = a_src[y]
    first.exchange()
    aa = fan("y", lambda k: a_src.at[hop(y, k)], lambda k: a_in.at[k], c_send.at[0], c_recv.at[0])
    rest.scatter()
    oc = []
    for k in range(4):
        if k > 0:
            ox[k - 1].wait_recv()
        got = o_big.at[:, pl.ds(3 * (lax.rem(xpos + 4 - k, 4) * 2 + core), 3)]
        oc.append(copy(got, got, o_send.at[1, 4 + k], o_recv.at[1, 4 + k], (s + 1 - 2 * core, m)))

    arrive(ta)
    obs_means = total(t_all, t_y[:, 0:8]) * (1.0 / GROUP)
    flat = jnp.concatenate([obs_means[:, b, :] for b in range(6)], axis=1)
    omean = jnp.mean(flat, axis=0, keepdims=True)
    apart = flat - omean
    for i in range(6):
        band = dot(apart[:, 128 * i : 128 * i + 128] * float(GROUP), apart[:, 0 : 128 * i + 128], (0, 0))
        for j in range(i + 1):
            at = 16 * BLOCKS.index((i, j))
            extra[at : at + 16] = band[:, 128 * j : 128 * j + 128].reshape(16, 8, 128)

    first.gather()
    rest.exchange()
    arrive(aa + oc)
    for k in range(SIDE):
        for b in range(6):
            lanes = slice(128 * b, 128 * b + 128)
            o_mat[32 * k : 32 * k + 32, lanes] = o_big[k, 4 * b : 4 * b + 4].reshape(MINE, 128) - omean[:, lanes]
    c_part[60:64] = jnp.zeros((4, 8, 128), F32)
    for b in range(6):
        band = dot(a_in[...].reshape(GROUP, 128), o_mat[:, 128 * b : 128 * b + 128], (0, 0))
        c_part[10 * b : 10 * b + 10] = band[0:SHARE].reshape(10, 8, 128)
    first.spread_chips()
    c1 = fan("z", lambda k: c_part.at[pl.ds(8 * hop(z, k), 8)], lambda k: c_one.at[k], c_send.at[1], c_recv.at[1])
    rest.gather()
    first.spread_cores()
    first.finish()

    scale = 1.0 / (MEMBERS - 1.0)
    part = lambda i: slice(128 * i, 128 * i + 128)
    diag = lax.broadcasted_iota(jnp.int32, (128, 128), 0) == lax.broadcasted_iota(jnp.int32, (128, 128), 1)

    def gram(i, j):
        at = 16 * BLOCKS.index((i, j))
        tiles = p_sum[at : at + 16] if at < 96 else r_sum[at - 96 : at - 80]
        return ((tiles + extra[at : at + 16]) * scale).reshape(128, 128)

    for i in range(3):
        s1[part(i), part(i)] = gram(i, i) + jnp.where(diag, var_ref[0:1, part(i)], 0.0)
        for j in range(i):
            block = gram(i, j)
            s1[part(i), part(j)] = block
            s1[part(j), part(i)] = block.T
    rest.spread_chips()
    sweep(s1, 0)
    rest.spread_cores()
    arrive(c1)
    piece = pl.ds(8 * z, 8)
    c_red[...] = total(c_one, c_part[piece])
    c_sum[piece] = c_red[...]
    c2 = fan("z", lambda k: c_red, lambda k: c_sum.at[piece], c_send.at[2], c_recv.at[2])
    sweep(s1, 1)
    sweep(s1, 2)
    rest.finish()
    for i in range(3):
        for j in range(3):
            f_ref[part(i), part(j)] = gram(3 + i, j)
    ut_ref[...] = dot(f_ref[...], s1[...])
    f_ref[...] = 0.75 * f_ref[...] + (0.25 * var_ref[0:1, :]) * ut_ref[...]
    for i in range(3):
        taken = dot(f_ref[part(i), :], ut_ref[0 : 128 * i + 128, :], (1, 1))
        for j in range(i + 1):
            block = gram(3 + i, 3 + j) - taken[:, part(j)]
            if i == j:
                s2[part(i), part(i)] = block + jnp.where(diag, var_ref[1:2, part(i)], 0.0)
            else:
                s2[part(i), part(j)] = block
                s2[part(j), part(i)] = block.T
    for p in range(3):
        sweep(s2, p)
    gap = jnp.concatenate([val_ref[0:1], val_ref[1:2]], axis=1) - omean
    arrive(c2)
    cross = jnp.concatenate([c_sum[10 * b : 10 * b + 10].reshape(SHARE, 128) for b in range(6)], axis=1) * scale
    v1 = dot(cross[:, :OBS], s1[...])
    v2 = dot(cross[:, OBS:] - dot(v1, f_ref[...], (1, 1)), s2[...])
    uv = dot(v2, ut_ref[...])
    shift = dot(jnp.broadcast_to(gap, (8, ALL)), jnp.concatenate([v1 - uv, v2], axis=1), (1, 1))
    spread = dot(o_mat[...], jnp.concatenate([0.5 * v1 - 0.25 * uv, 0.5 * v2], axis=1), (1, 1))
    gain = shift[0:1] - spread
    for k in range(SIDE):
        d_src[k, :, 0:SHARE] = gain[32 * k : 32 * k + 32]
        d_src[k, :, SHARE:128] = jnp.zeros((MINE, 128 - SHARE), F32)
    d_in[y] = d_src[0]
    back = fan("y", lambda k: d_src.at[SIDE - k], lambda k: d_in.at[y], c_send.at[3], c_recv.at[3])
    for c in started[: 1 - SIDE]:
        c.wait_send()
    arrive(back)
    for c in range(SIDE):
        lanes = slice(SHARE * c, SHARE * c + SHARE)
        out_ref[:, lanes] = x_ref[:, lanes] + d_in[c, :, 0:SHARE]
    done = pltpu.make_async_copy(out_ref, out_hbm, in_sem.at[5])
    done.start()
    for c in back:
        c.wait_send()
    done.wait()


def shards(state, obs_values, noise_var, obs_rows, owner):
    dma = pltpu.SemaphoreType.DMA
    plane = lambda rows, cols: pltpu.VMEM((rows, cols), F32)
    tiles = lambda *lead: pltpu.VMEM((*lead, 8, 128), F32)
    return pl.pallas_call(
        kernel,
        out_shape=jax.ShapeDtypeStruct((MINE, ROWS), F32),
        in_specs=[pl.BlockSpec(memory_space=pl.ANY)] * 5,
        out_specs=pl.BlockSpec(memory_space=pl.ANY),
        scratch_shapes=[
            plane(MINE, ROWS), plane(2, OBS), plane(2, OBS), pltpu.VMEM((2, OBS), jnp.int32), pltpu.VMEM((2, 3), jnp.int32),
            plane(MINE, ROWS),
            plane(MINE, ALL), plane(OBS, OBS), plane(OBS, OBS), plane(OBS, OBS), plane(OBS, OBS), tiles(336),
            plane(16, 128), pltpu.VMEM((SIDE, 16, 128), F32), pltpu.VMEM((SIDE, 16, 128), F32), tiles(SIDE), tiles(SIDE, SIDE),
            tiles(24), tiles(SIDE, 3), tiles(3), tiles(24),
            tiles(128), tiles(2, SIDE, 1), tiles(2, SIDE, 1), tiles(2, 1), tiles(128),
            tiles(256), tiles(2, SIDE, 2), tiles(2, SIDE, 2), tiles(2, 2), tiles(256),
            tiles(SIDE, 24), plane(GROUP, ALL), pltpu.VMEM((SIDE, MINE, 128), F32), pltpu.VMEM((SIDE, MINE, 128), F32),
            tiles(64), tiles(SIDE, 8), tiles(8), tiles(64),
            pltpu.VMEM((SIDE, MINE, 128), F32), pltpu.VMEM((SIDE, MINE, 128), F32),
            dma((6,)), dma((4, SIDE)), dma((4, SIDE)), dma((2, SIDE)), dma((2, SIDE)),
            dma((2, 3, SIDE)), dma((2, 3, SIDE)), dma((2, 3, SIDE)), dma((2, 3, SIDE)),
            dma((2, SIDE)), dma((2, SIDE)), dma((2, SIDE)), dma((2, SIDE)), dma((4, SIDE)), dma((4, SIDE)),
        ],
        compiler_params=pltpu.CompilerParams(
            collective_id=0, has_side_effects=True, vmem_limit_bytes=40 * 2**20
        ),
    )(state, obs_values, noise_var, obs_rows, owner)


def solution(mesh):
    placed = (P("member", "state"), P(), P(), P(), P())
    return jax.shard_map(
        shards, mesh=mesh, in_specs=placed, out_specs=P("member", "state"), check_vma=False
    )
```

```python
import functools

import jax
import jax.numpy as jnp
from jax import lax
from jax.experimental import pallas as pl
from jax.experimental.pallas import tpu as pltpu
from jax.sharding import PartitionSpec as P

MESH = pl.DeviceIdType.MESH
F32 = jnp.float32
HIGHEST = lax.Precision.HIGHEST
SIDE = 8
OBS = 384
ALL = 2 * OBS
ROWS = 640
MINE = 32
MEMBERS = 2048
GROUP = MINE * SIDE
SHARE = ROWS // SIDE
BLOCKS = [(i, j) for i in range(6) for j in range(i + 1)]
HALVES = (0, 1)


def dot(a, b, over=(1, 0)):
    return lax.dot_general(
        a, b, (((over[0],), (over[1],)), ((), ())), precision=HIGHEST, preferred_element_type=F32
    )


def total(slots, own):
    out = own
    for k in range(1, SIDE):
        out = out + slots[k]
    return out


def eliminate(ref, at):
    spread = functools.partial(jnp.broadcast_to, shape=(8, 128))
    lane = lax.broadcasted_iota(jnp.int32, (8, 128), 1)
    sub = lax.broadcasted_iota(jnp.int32, (8, 128), 0)
    a = [ref[at + 8 * i : at + 8 * i + 8, at : at + 128] for i in range(16)]
    for p in range(16):
        rows = a[p]
        cols = [spread(rows[:, 8 * p + j : 8 * p + j + 1]) for j in range(8)]
        for k in range(8):
            col = cols[k]
            pivot = 1.0 / spread(col[k : k + 1])
            rows = jnp.where(lane == 8 * p + k, jnp.where(sub == k, 1.0, 0.0), rows)
            times = jnp.where(sub == k, 1.0 - pivot, col * pivot)
            for j in range(k + 1, 8):
                cols[j] = cols[j] - times * spread(cols[j][k : k + 1])
            rows = rows - times * spread(rows[k : k + 1])
        each = [spread(rows[j : j + 1]) for j in range(8)]
        inside = (lane >= 8 * p) & (lane < 8 * p + 8)
        for i in [(p + 1 + i) % 16 for i in range(15)]:
            old = a[i]
            t = [spread(old[:, 8 * p + j : 8 * p + j + 1]) * each[j] for j in range(8)]
            low, high = (t[0] + t[1]) + (t[2] + t[3]), (t[4] + t[5]) + (t[6] + t[7])
            a[i] = jnp.where(inside, 0.0, old) - (low + high)
        a[p] = rows
    for i in range(16):
        ref[at + 8 * i : at + 8 * i + 8, at : at + 128] = a[i]


def sweep(ref, p):
    part = lambda i: slice(128 * i, 128 * i + 128)
    eliminate(ref, 128 * p)
    inner = ref[part(p), part(p)]
    others = [(p + 1) % 3, (p + 2) % 3]
    for j in others:
        ref[part(p), part(j)] = dot(inner, ref[part(p), part(j)])
    for i in others:
        left = ref[part(i), part(p)]
        for j in others:
            ref[part(i), part(j)] -= dot(left, ref[part(p), part(j)])
        ref[part(i), part(p)] = -dot(left, inner)


def kernel(
    x_hbm, small_hbm, out_hbm,
    x_ref, small_ref, out_ref,
    oa_ref, s1, s2, ut_ref, f_ref, extra,
    t_in, t_z, t_y, t_s, t_all, l_src, l_in, l_mine, l_all,
    p_part, p_one, p_two, p_red, p_sum, r_part, r_one, r_two, r_red, r_sum,
    o_big, o_mat, a_src, a_in, c_part, c_one, c_red, c_sum, d_src, d_in,
    in_sem, t_send, t_recv, l_send, l_recv, p_send, p_recv, r_send, r_recv, x_send, x_recv, o_send, o_recv, c_send, c_recv,
):
    s = lax.axis_index("state")
    m = lax.axis_index("member")
    z, y = lax.div(m, SIDE), lax.rem(m, SIDE)
    xpos, core = lax.div(s, 2), lax.rem(s, 2)

    def hop(v, k):
        return lax.rem(v + k, SIDE)

    def peer(axis, k):
        if axis == "z":
            return (s, hop(z, k) * SIDE + y)
        if axis == "y":
            return (s, z * SIDE + hop(y, k))
        return (hop(s, k), m)

    loads = []
    pairs = ((x_hbm, x_ref), (small_hbm, small_ref))
    for i, (src, dst) in enumerate(pairs):
        c = pltpu.make_async_copy(src, dst, in_sem.at[i])
        c.start()
        loads.append(c)
    barrier = pltpu.get_barrier_semaphore()
    for axis in ("z", "y", "s"):
        for k in range(1, SIDE):
            pl.semaphore_signal(barrier, inc=1, device_id=peer(axis, k), device_id_type=MESH)

    started = []

    def copy(src, dst, send, recv, where):
        c = pltpu.make_async_remote_copy(
            src_ref=src, dst_ref=dst, send_sem=send, recv_sem=recv, device_id=where, device_id_type=MESH
        )
        c.start()
        started.append(c)
        return c

    def arrive(copies):
        for c in copies:
            c.wait_recv()

    def fan(axis, src, dst, send, recv, over=(4, 3, 5, 2, 6, 1, 7)):
        return [copy(src(k), dst(k), send.at[k], recv.at[k], peer(axis, k)) for k in over]

    for c in loads:
        c.wait()
    x = x_ref[...]
    iota = lax.broadcasted_iota(jnp.int32, (ROWS, 128), 0).astype(F32)
    t_in[...] = jnp.zeros_like(t_in)
    for b in range(6):
        want = small_ref[4 + b // 3 : 5 + b // 3, 128 * (b % 3) : 128 * (b % 3) + 128]
        rows = dot(x, jnp.where(iota == want, 1.0, 0.0))
        t_in[b : b + 1, :] = jnp.sum(rows, axis=0, keepdims=True)
        l_src[4 * b : 4 * b + 4] = rows.reshape(4, 8, 128)
    sx = jnp.sum(x, axis=0, keepdims=True)
    for b in range(5):
        t_in[8 + b : 9 + b, :] = sx[:, 128 * b : 128 * b + 128]
    pl.semaphore_wait(barrier, 3 * (SIDE - 1))

    tz = fan("z", lambda k: t_in, lambda k: t_z.at[k], t_send.at[0], t_recv.at[0])
    ls = fan("s", lambda k: l_src.at[pl.ds(3 * hop(s, k), 3)], lambda k: l_in.at[k], l_send.at[0], l_recv.at[0])
    arrive(ls)
    l_mine[...] = total(l_in, l_src[pl.ds(3 * s, 3)])
    l_all[pl.ds(3 * s, 3)] = l_mine[...]
    la = fan("s", lambda k: l_mine, lambda k: l_all.at[pl.ds(3 * s, 3)], l_send.at[1], l_recv.at[1])
    mine = pl.ds(3 * s, 3)
    o_big[0, mine] = l_mine[...]
    ya = fan("y", lambda k: l_mine, lambda k: o_big.at[k, mine], o_send.at[0], o_recv.at[0])
    arrive(tz)
    t_y[0] = total(t_z, t_in[...])
    ts = fan("s", lambda k: t_y.at[0, 0:8], lambda k: t_s.at[k], t_send.at[1], t_recv.at[1])
    ty = fan("y", lambda k: t_y.at[0], lambda k: t_y.at[k], t_send.at[2], t_recv.at[2])
    arrive(la)
    arrive(ts)
    onear = total(t_s, t_y[0, 0:8]) * (1.0 / GROUP)
    for b in range(6):
        oa_ref[:, 128 * b : 128 * b + 128] = l_all[4 * b : 4 * b + 4].reshape(MINE, 128) - onear[b : b + 1]

    order = (("z", z, "y", y), ("y", y, "z", z))

    class Gram:
        def __init__(self, n, part, one, two, red, out, send, recv, at):
            self.n, self.part, self.one, self.two, self.red, self.out = n, part, one, two, red, out
            self.send, self.recv, self.at = send, recv, at
            self.base = s * (16 * n)

        def piece(self, h, place):
            return pl.ds(self.base + 8 * self.n * h + self.n * place, self.n)

        def scatter(self):
            self.now = [
                fan(
                    order[h][0],
                    lambda k: self.part.at[self.piece(h, hop(order[h][1], k))],
                    lambda k: self.one.at[h, k],
                    self.send.at[h, 0],
                    self.recv.at[h, 0],
                )
                for h in HALVES
            ]

        def exchange(self):
            after = []
            for h in HALVES:
                arrive(self.now[h])
                self.two[h, 0] = total(self.one.at[h], self.part[self.piece(h, order[h][1])])
                after.append(
                    fan(
                        order[h][2],
                        lambda k: self.two.at[h, 0],
                        lambda k: self.two.at[h, k],
                        self.send.at[h, 1],
                        self.recv.at[h, 1],
                    )
                )
            self.now = after

        def gather(self):
            after = []
            for h in HALVES:
                arrive(self.now[h])
                self.red[h] = total(self.two.at[h], self.two[h, 0])
                piece = self.piece(h, order[h][1])
                self.out[piece] = self.red[h]
                after.append(
                    fan(
                        order[h][0],
                        lambda k: self.red.at[h],
                        lambda k: self.out.at[piece],
                        self.send.at[h, 2],
                        self.recv.at[h, 2],
                    )
                )
            self.now = after

        def spread_chips(self):
            arrive(self.now[0] + self.now[1])
            mine = self.out.at[pl.ds(self.base, 16 * self.n)]
            self.now = [
                copy(mine, mine, x_send.at[self.at, k], x_recv.at[self.at, k], (lax.rem(xpos + k, 4) * 2 + core, m))
                for k in range(1, 4)
            ]

        def spread_cores(self):
            after = []
            for k in range(4):
                if k > 0:
                    self.now[k - 1].wait_recv()
                got = self.out.at[pl.ds((lax.rem(xpos + 4 - k, 4) * 2 + core) * (16 * self.n), 16 * self.n)]
                after.append(
                    copy(got, got, x_send.at[self.at, 4 + k], x_recv.at[self.at, 4 + k], (s + 1 - 2 * core, m))
                )
            self.now = after

        def finish(self):
            arrive(self.now)

    first = Gram(1, p_part, p_one, p_two, p_red, p_sum, p_send, p_recv, 0)
    rest = Gram(2, r_part, r_one, r_two, r_red, r_sum, r_send, r_recv, 1)

    def bands(which, into, skip):
        for i in which:
            band = dot(oa_ref[:, 128 * i : 128 * i + 128], oa_ref[:, 0 : 128 * i + 128], (0, 0))
            for j in range(i + 1):
                at = 16 * (BLOCKS.index((i, j)) - skip)
                into[at : at + 16] = band[:, 128 * j : 128 * j + 128].reshape(16, 8, 128)

    bands(range(3), p_part, 0)
    p_part[96:128] = jnp.zeros((32, 8, 128), F32)
    first.scatter()
    bands(range(3, 6), r_part, 6)
    r_part[240:256] = jnp.zeros((16, 8, 128), F32)
    arrive(ya)
    ox = [
        copy(
            o_big.at[:, mine],
            o_big.at[:, mine],
            o_send.at[1, k],
            o_recv.at[1, k],
            (lax.rem(xpos + k, 4) * 2 + core, m),
        )
        for k in range(1, 4)
    ]
    arrive(ty)
    ta = fan("s", lambda k: t_y.at[:, 0:8], lambda k: t_all.at[k], t_send.at[3], t_recv.at[3])
    row_means = sum(t_y[k, 8:16] for k in range(SIDE)) * (1.0 / MEMBERS)
    about = x - jnp.concatenate([row_means[b : b + 1] for b in range(5)], axis=1)
    a_src[...] = jnp.zeros_like(a_src)
    for c in range(SIDE):
        a_src[c, :, 0:SHARE] = about[:, SHARE * c : SHARE * c + SHARE]
    a_in[0] = a_src[y]
    first.exchange()
    aa = fan("y", lambda k: a_src.at[hop(y, k)], lambda k: a_in.at[k], c_send.at[0], c_recv.at[0])
    rest.scatter()
    oc = []
    for k in range(4):
        if k > 0:
            ox[k - 1].wait_recv()
        got = o_big.at[:, pl.ds(3 * (lax.rem(xpos + 4 - k, 4) * 2 + core), 3)]
        oc.append(copy(got, got, o_send.at[1, 4 + k], o_recv.at[1, 4 + k], (s + 1 - 2 * core, m)))

    arrive(ta)
    obs_means = total(t_all, t_y[:, 0:8]) * (1.0 / GROUP)
    flat = jnp.concatenate([obs_means[:, b, :] for b in range(6)], axis=1)
    omean = jnp.mean(flat, axis=0, keepdims=True)
    apart = flat - omean
    for i in range(6):
        band = dot(apart[:, 128 * i : 128 * i + 128] * float(GROUP), apart[:, 0 : 128 * i + 128], (0, 0))
        for j in range(i + 1):
            at = 16 * BLOCKS.index((i, j))
            extra[at : at + 16] = band[:, 128 * j : 128 * j + 128].reshape(16, 8, 128)

    first.gather()
    rest.exchange()
    arrive(aa + oc)
    for k in range(SIDE):
        for b in range(6):
            lanes = slice(128 * b, 128 * b + 128)
            o_mat[32 * k : 32 * k + 32, lanes] = o_big[k, 4 * b : 4 * b + 4].reshape(MINE, 128) - omean[:, lanes]
    c_part[60:64] = jnp.zeros((4, 8, 128), F32)
    for b in range(6):
        band = dot(a_in[...].reshape(GROUP, 128), o_mat[:, 128 * b : 128 * b + 128], (0, 0))
        c_part[10 * b : 10 * b + 10] = band[0:SHARE].reshape(10, 8, 128)
    first.spread_chips()
    c1 = fan("z", lambda k: c_part.at[pl.ds(8 * hop(z, k), 8)], lambda k: c_one.at[k], c_send.at[1], c_recv.at[1])
    rest.gather()
    first.spread_cores()
    first.finish()

    scale = 1.0 / (MEMBERS - 1.0)
    part = lambda i: slice(128 * i, 128 * i + 128)
    diag = lax.broadcasted_iota(jnp.int32, (128, 128), 0) == lax.broadcasted_iota(jnp.int32, (128, 128), 1)

    def gram(i, j):
        at = 16 * BLOCKS.index((i, j))
        tiles = p_sum[at : at + 16] if at < 96 else r_sum[at - 96 : at - 80]
        return ((tiles + extra[at : at + 16]) * scale).reshape(128, 128)

    for i in range(3):
        s1[part(i), part(i)] = gram(i, i) + jnp.where(diag, small_ref[2:3, part(i)], 0.0)
        for j in range(i):
            block = gram(i, j)
            s1[part(i), part(j)] = block
            s1[part(j), part(i)] = block.T
    rest.spread_chips()
    sweep(s1, 0)
    rest.spread_cores()
    arrive(c1)
    piece = pl.ds(8 * z, 8)
    c_red[...] = total(c_one, c_part[piece])
    c_sum[piece] = c_red[...]
    c2 = fan("z", lambda k: c_red, lambda k: c_sum.at[piece], c_send.at[2], c_recv.at[2])
    sweep(s1, 1)
    sweep(s1, 2)
    rest.finish()
    for i in range(3):
        for j in range(3):
            f_ref[part(i), part(j)] = gram(3 + i, j)
    ut_ref[...] = dot(f_ref[...], s1[...])
    f_ref[...] = 0.75 * f_ref[...] + (0.25 * small_ref[2:3, :]) * ut_ref[...]
    for i in range(3):
        taken = dot(f_ref[part(i), :], ut_ref[0 : 128 * i + 128, :], (1, 1))
        for j in range(i + 1):
            block = gram(3 + i, 3 + j) - taken[:, part(j)]
            if i == j:
                s2[part(i), part(i)] = block + jnp.where(diag, small_ref[3:4, part(i)], 0.0)
            else:
                s2[part(i), part(j)] = block
                s2[part(j), part(i)] = block.T
    for p in range(3):
        sweep(s2, p)
    gap = jnp.concatenate([small_ref[0:1], small_ref[1:2]], axis=1) - omean
    arrive(c2)
    cross = jnp.concatenate([c_sum[10 * b : 10 * b + 10].reshape(SHARE, 128) for b in range(6)], axis=1) * scale
    v1 = dot(cross[:, :OBS], s1[...])
    v2 = dot(cross[:, OBS:] - dot(v1, f_ref[...], (1, 1)), s2[...])
    uv = dot(v2, ut_ref[...])
    shift = dot(jnp.broadcast_to(gap, (8, ALL)), jnp.concatenate([v1 - uv, v2], axis=1), (1, 1))
    spread = dot(o_mat[...], jnp.concatenate([0.5 * v1 - 0.25 * uv, 0.5 * v2], axis=1), (1, 1))
    gain = shift[0:1] - spread
    for k in range(SIDE):
        d_src[k, :, 0:SHARE] = gain[32 * k : 32 * k + 32]
        d_src[k, :, SHARE:128] = jnp.zeros((MINE, 128 - SHARE), F32)
    d_in[y] = d_src[0]
    back = fan("y", lambda k: d_src.at[SIDE - k], lambda k: d_in.at[y], c_send.at[3], c_recv.at[3])
    for c in started[: 1 - SIDE]:
        c.wait_send()
    arrive(back)
    for c in range(SIDE):
        lanes = slice(SHARE * c, SHARE * c + SHARE)
        out_ref[:, lanes] = x_ref[:, lanes] + d_in[c, :, 0:SHARE]
    done = pltpu.make_async_copy(out_ref, out_hbm, in_sem.at[5])
    done.start()
    for c in back:
        c.wait_send()
    done.wait()


def shards(state, obs_values, noise_var, obs_rows, owner):
    held = jnp.repeat(owner == lax.axis_index("state"), 128, axis=1)
    want = jnp.where(held, obs_rows, -1).astype(F32)
    small = jnp.concatenate([obs_values, noise_var, want, jnp.zeros_like(want)], axis=0)
    dma = pltpu.SemaphoreType.DMA
    plane = lambda rows, cols: pltpu.VMEM((rows, cols), F32)
    tiles = lambda *lead: pltpu.VMEM((*lead, 8, 128), F32)
    return pl.pallas_call(
        kernel,
        out_shape=jax.ShapeDtypeStruct((MINE, ROWS), F32),
        in_specs=[pl.BlockSpec(memory_space=pl.ANY)] * 2,
        out_specs=pl.BlockSpec(memory_space=pl.ANY),
        scratch_shapes=[
            plane(MINE, ROWS), plane(8, OBS), plane(MINE, ROWS),
            plane(MINE, ALL), plane(OBS, OBS), plane(OBS, OBS), plane(OBS, OBS), plane(OBS, OBS), tiles(336),
            plane(16, 128), pltpu.VMEM((SIDE, 16, 128), F32), pltpu.VMEM((SIDE, 16, 128), F32), tiles(SIDE), tiles(SIDE, SIDE),
            tiles(24), tiles(SIDE, 3), tiles(3), tiles(24),
            tiles(128), tiles(2, SIDE, 1), tiles(2, SIDE, 1), tiles(2, 1), tiles(128),
            tiles(256), tiles(2, SIDE, 2), tiles(2, SIDE, 2), tiles(2, 2), tiles(256),
            tiles(SIDE, 24), plane(GROUP, ALL), pltpu.VMEM((SIDE, MINE, 128), F32), pltpu.VMEM((SIDE, MINE, 128), F32),
            tiles(64), tiles(SIDE, 8), tiles(8), tiles(64),
            pltpu.VMEM((SIDE, MINE, 128), F32), pltpu.VMEM((SIDE, MINE, 128), F32),
            dma((6,)), dma((4, SIDE)), dma((4, SIDE)), dma((2, SIDE)), dma((2, SIDE)),
            dma((2, 3, SIDE)), dma((2, 3, SIDE)), dma((2, 3, SIDE)), dma((2, 3, SIDE)),
            dma((2, SIDE)), dma((2, SIDE)), dma((2, SIDE)), dma((2, SIDE)), dma((4, SIDE)), dma((4, SIDE)),
        ],
        compiler_params=pltpu.CompilerParams(
            collective_id=0, has_side_effects=True, vmem_limit_bytes=40 * 2**20
        ),
    )(state, small)


def solution(mesh):
    placed = (P("member", "state"), P(), P(), P(), P())
    return jax.shard_map(
        shards, mesh=mesh, in_specs=placed, out_specs=P("member", "state"), check_vma=False
    )
```
